32 devices in a mesh: dom: 16 (over z, y, x), orb: 2 (over core).
Axes of the slice: x: 2, y: 2, z: 4, core: 2. Of those that a mesh axis runs over, the one named last changes fastest.
Arguments:
- block: float32 [256, 10816], P('orb', 'dom')
- conn: int32 [125, 144], P(None, 'dom'), may hold values from 0 to 844, as said below
- bottom: int32 [2704], P('dom'), may hold values from 0 to 675, as said below
- cell_scale: float32 [144], P('dom'), may hold values from 0.5 to 2
- potential: float32 [216, 144], P(None, 'dom'), may hold values from 0.1 to 1
- mass: float32 [10816], P('dom'), may hold values from 0.5 to 2
- stiffness: float32 [125, 125], replicated, as said below
- interp: float32 [216, 125], replicated, may hold values from -0.5 to 0.5
- occupancy: float32 [256], P('orb'), may hold values from 0.2 to 2
- spectrum: float32 [2], replicated, as said below
Outputs:
- density: float32 [216, 144], P(None, 'dom')
The draws below stay inside these ranges and needn't reach their ends.
Inputs may be any that keep to these rules, and one draw needn't show every extreme that they name: `conn`: for the cells of domain d an entry below 676 is one of d's own local node numbers and 676 + f names entry f of the next domain's list in bottom; every own node is named by some cell of its domain, and the cells form a conforming mesh. `bottom`: each domain's 169 entries are distinct local numbers of its own nodes. `stiffness`: symmetric and positive definite. spectrum[0] < spectrum[1].
All inputs are finite; a program needn't handle non-finite values.
Results may differ from the reference program's by a relative error of at most 0.0001.
Values sent between devices are 32-bit elements; how exact they have to be, the bound alone decides.
A program may use at most 64 MiB of HBM per device.

```python
import math
import jax
import jax.numpy as jnp
from jax import lax

ORBS = 256
GRID = 3
LAYERS = 1
DEG = 3
NPC = 125
GAUSS = 216
FACE = 169
NODE_DEV = 676
CELL_DEV = 9
CELLS = 144
NODES = 10816


def relabel_nodes(lone_element):
    rest = 1 + jax.random.permutation(lone_element, NODE_DEV - 2).astype(jnp.int32)
    ends = jnp.array([NODE_DEV - 1, 0], dtype=jnp.int32)
    return jnp.concatenate([ends, rest])


def mesh_tables(key):
    ndom = CELLS // CELL_DEV
    side = 4 * GRID + 1
    random_keys = jax.random.split(jax.random.fold_in(key, 17), ndom)
    sort_orders = jax.vmap(relabel_nodes)(random_keys).astype(jnp.int32)
    cell = jnp.arange(CELL_DEV, dtype=jnp.int32)
    corner_x = 4 * (cell % GRID)
    vertex_y_coord = 4 * (cell // GRID % GRID)
    vertex_z_coord = 4 * (cell // (GRID * GRID))
    local = jnp.arange(NPC, dtype=jnp.int32)
    node_x = corner_x[None, :] + local[:, None] % 5
    node_y = vertex_y_coord[None, :] + local[:, None] // 5 % 5
    node_z = vertex_z_coord[None, :] + local[:, None] // 25
    drawn = (node_z * side + node_y) * side + node_x
    ghost = NODE_DEV + node_y * side + node_x
    inside = node_z < 4 * LAYERS
    renamed = sort_orders[:, jnp.minimum(drawn, NODE_DEV - 1)]
    linked = jnp.where(inside[None], renamed, ghost[None])
    linked = jnp.transpose(linked, (1, 0, 2)).reshape(NPC, ndom * CELL_DEV)
    shared = sort_orders[:, jnp.arange(side * side, dtype=jnp.int32)].reshape(ndom * side * side)
    return (linked, shared)


def draw_conn(key, part):
    return mesh_tables(key)[0]


def draw_bottom(key, part):
    return mesh_tables(key)[1]


def draw_block(key, part):
    ndom = NODES // NODE_DEV
    first, second, third = jax.random.split(jax.random.fold_in(key, 3), 3)
    noise = jnp.clip(jax.random.normal(first, (ORBS, NODES), jnp.float32), -5.0, 5.0)
    common = jnp.clip(jax.random.normal(second, (NODES,), jnp.float32), -5.0, 5.0)
    loading = jax.random.uniform(third, (ORBS,), jnp.float32, 0.3, 1.0)
    domain = (jnp.arange(NODES, dtype=jnp.int32) // NODE_DEV).astype(jnp.float32)
    ramp = 1.0 + 2.0 * domain / max(ndom - 1, 1)
    return (noise + loading[:, None] * common[None, :]) * ramp[None, :]


def draw_stiffness(key, part):
    first, second = jax.random.split(jax.random.fold_in(key, 5), 2)
    raw = jax.random.uniform(first, (NPC, NPC), jnp.float32, -1.0, 1.0) * (1.5 / NPC)
    offdiag = (raw + raw.T) * 0.5 * (1.0 - jnp.eye(NPC, dtype=jnp.float32))
    diagonal = jax.random.uniform(second, (NPC,), jnp.float32, 1.5, 2.0)
    return offdiag + jnp.diag(diagonal)


def draw_spectrum(key, part):
    unit = jax.random.uniform(jax.random.fold_in(key, 7), (2,), jnp.float32, 0.0, 1.0)
    return jnp.stack([2.0 + 2.0 * unit[0], 40.0 + 20.0 * unit[1]])


def steps_of(rng, dims, shards, least, top_value):
    factor_of = 1.0
    for dim, blocks in shards:
        steps = jax.random.uniform(jax.random.fold_in(jax.random.fold_in(rng, 6), dim), (blocks,), jnp.float32, least / len(shards), top_value / len(shards))
        factor_of = factor_of * jnp.repeat(jnp.exp(steps), dims[dim] // blocks).reshape((-1,) + (1,) * (len(dims) - 1 - dim))
    return factor_of


def bell_draw(stream_key, dims, width, limit, kind=jnp.bfloat16):
    entries = width * jax.random.normal(stream_key, dims, jnp.float32)
    return jnp.clip(entries, min=-limit, max=limit).astype(kind)


def setup_inputs(seed: int = 0) -> dict:
    arg_keys = jax.random.split(jax.random.key(seed), 11)
    return {
        "block": draw_block(jax.random.fold_in(arg_keys[10], 71), 0),
        "conn": draw_conn(jax.random.fold_in(arg_keys[10], 71), 0),
        "bottom": draw_bottom(jax.random.fold_in(arg_keys[10], 71), 0),
        "cell_scale": jnp.clip(jnp.exp(math.log(2.0) - 1.3862944 * jax.random.uniform(arg_keys[3], (CELLS,), jnp.float32) ** steps_of(arg_keys[3], (CELLS,), ((0, 16),), -0.2, 0.2)), 0.5, 2.0),
        "potential": jnp.clip(jnp.exp(math.log(1.0) - 2.3025851 * jax.random.uniform(arg_keys[4], (GAUSS, CELLS), jnp.float32) ** steps_of(arg_keys[4], (GAUSS, CELLS), ((1, 16),), -0.2, 0.2)), 0.1, 1.0),
        "mass": jnp.clip(jnp.exp(math.log(2.0) - 1.3862944 * jax.random.uniform(arg_keys[5], (NODES,), jnp.float32) ** steps_of(arg_keys[5], (NODES,), ((0, 16),), -0.2, 0.2)), 0.5, 2.0),
        "stiffness": draw_stiffness(jax.random.fold_in(arg_keys[10], 71), 0),
        "interp": bell_draw(arg_keys[7], (GAUSS, NPC), NPC ** -0.5, 0.5, jnp.float32),
        "occupancy": jnp.clip(0.2 + 1.8 * jax.random.uniform(arg_keys[8], (ORBS,), jnp.float32) ** steps_of(arg_keys[8], (ORBS,), ((0, 2),), -0.2, 0.2), 0.2, 2.0),
        "spectrum": draw_spectrum(jax.random.fold_in(arg_keys[10], 71), 0),
    }


def cell_values(ext, conn):
    orbs = ext.shape[0]
    npc, cells = conn.shape
    picked = jnp.take(ext, conn.reshape(-1), axis=1).reshape(orbs, npc, cells)
    return jnp.transpose(picked, (1, 0, 2)).reshape(npc, orbs * cells)

def cell_apply(ext, conn, cell_scale, potential, stiffness, interp):
    orbs = ext.shape[0]
    npc, cells = conn.shape
    local = cell_values(ext, conn)
    stiff = jnp.dot(stiffness.astype(jnp.float32), local.astype(jnp.float32), precision=lax.Precision.HIGHEST, preferred_element_type=jnp.float32)
    quad = jnp.dot(interp.astype(jnp.float32), local.astype(jnp.float32), precision=lax.Precision.HIGHEST, preferred_element_type=jnp.float32)
    quad = quad.reshape(-1, orbs, cells) * potential[:, None, :]
    back = jnp.dot(interp.T.astype(jnp.float32), quad.reshape(-1, orbs * cells).astype(jnp.float32), precision=lax.Precision.HIGHEST, preferred_element_type=jnp.float32)
    total = stiff.reshape(npc, orbs, cells) * cell_scale[None, None, :] + back.reshape(npc, orbs, cells)
    values = jnp.transpose(total, (1, 0, 2)).reshape(orbs, npc * cells)
    return jnp.zeros_like(ext).at[:, conn.reshape(-1)].add(values)

def density_terms(ext, conn, interp, occupancy):
    orbs = ext.shape[0]
    npc, cells = conn.shape
    local = cell_values(ext, conn)
    quad = jnp.dot(interp.astype(jnp.float32), local.astype(jnp.float32), precision=lax.Precision.HIGHEST, preferred_element_type=jnp.float32)
    quad = quad.reshape(-1, orbs, cells)
    return jnp.sum(occupancy[None, :, None] * quad * quad, axis=1) / ORBS

def widen_matrix(field, bottom_d):
    faces = jax.vmap(lambda part, rows: part[:, rows])(field, bottom_d)
    ghost = jnp.concatenate([faces[1:], jnp.zeros_like(faces[:1])], axis=0)
    return jnp.concatenate([field, ghost], axis=2)

def apply_all(field, conn_d, scale_d, pot_d, bottom_d, mass_d, stiffness, interp):
    ext = widen_matrix(field, bottom_d)
    partial_value = lax.map(lambda items: cell_apply(items[0], items[1], items[2], items[3], stiffness, interp), (ext, conn_d, scale_d, pot_d))
    owned = partial_value[:, :, :NODE_DEV]
    rims = partial_value[:, :, NODE_DEV:]
    incoming = jnp.concatenate([jnp.zeros_like(rims[:1]), rims[:-1]], axis=0)
    owned = jax.vmap(lambda part, rows, extra: part.at[:, rows].add(extra))(owned, bottom_d, incoming)
    return owned / mass_d[:, None, :]

def reference(block, conn, bottom, cell_scale, potential, mass, stiffness, interp, occupancy, spectrum):
    ndom = cell_scale.shape[0] // CELL_DEV
    field = jnp.transpose(block.reshape(ORBS, ndom, NODE_DEV), (1, 0, 2))
    conn_d = jnp.transpose(conn.reshape(NPC, ndom, CELL_DEV), (1, 0, 2))
    pot_d = jnp.transpose(potential.reshape(GAUSS, ndom, CELL_DEV), (1, 0, 2))
    scale_d = cell_scale.reshape(ndom, CELL_DEV)
    bottom_d = bottom.reshape(ndom, FACE)
    mass_d = mass.reshape(ndom, NODE_DEV)
    halfwidth = (spectrum[1] - spectrum[0]) / 2.0
    centre = (spectrum[1] + spectrum[0]) / 2.0

    def operator(values):
        return apply_all(values, conn_d, scale_d, pot_d, bottom_d, mass_d, stiffness, interp)
    previous = field
    current = (operator(field) - centre * field) / halfwidth
    for step in range(DEG - 1):
        following = 2.0 * (operator(current) - centre * current) / halfwidth - previous
        previous = current
        current = following
    gram = jnp.einsum('dok,dpk->op', current * mass_d[:, None, :], current, precision=lax.Precision.HIGHEST) / (ndom * NODE_DEV)
    multiplier = jnp.linalg.cholesky(gram)
    inverse = jax.scipy.linalg.solve_triangular(multiplier, jnp.eye(ORBS, dtype=jnp.float32), lower=True)
    ortho = jnp.einsum('op,dpn->don', inverse, current, precision=lax.Precision.HIGHEST)
    ext = widen_matrix(ortho, bottom_d)
    dens = lax.map(lambda items: density_terms(items[0], items[1], interp, occupancy), (ext, conn_d))
    return jnp.transpose(dens, (1, 0, 2)).reshape(GAUSS, ndom * CELL_DEV)
```

```python
import functools

import jax
import jax.numpy as jnp
from jax import lax
from jax.experimental import pallas as pl
from jax.experimental.pallas import tpu as pltpu
from jax.sharding import PartitionSpec as P

DEG = 3
LANE = 128
PAD = 256
HI = lax.Precision.HIGHEST
MESH = pl.DeviceIdType.MESH
F32 = jnp.float32
BF16 = jnp.bfloat16
NN = (((1,), (0,)), ((), ()))
NT = (((1,), (1,)), ((), ()))
TN = (((0,), (0,)), ((), ()))
VLIMIT = 48 * 1024 * 1024


def up(value, unit):
    return -(-value // unit) * unit


def full_dot(left, right, dims=NN):
    return lax.dot_general(left, right, dims, precision=HI, preferred_element_type=F32)


def split3(value):
    high = value.astype(BF16)
    rest = value - high.astype(F32)
    mid = rest.astype(BF16)
    low = (rest - mid.astype(F32)).astype(BF16)
    return high, mid, low


def pick_dot(left, onehot, dims=NN):
    high, mid, low = (
        lax.dot_general(part, onehot, dims, preferred_element_type=F32) for part in split3(left)
    )
    return (low + mid) + high


def assemble_kernel(conn_ref, scale_ref, pot_ref, stiff_ref, interp_ref, a_ref, gt_ref, w_ref):
    ext = a_ref.shape[0]
    cells = conn_ref.shape[0]
    interp = interp_ref[...]
    rows = lax.broadcasted_iota(jnp.int32, (ext, LANE), 0)
    for cell in range(cells):
        cols = slice(cell * LANE, (cell + 1) * LANE)
        hot = (rows == conn_ref[cell : cell + 1, :]).astype(F32).astype(BF16)
        gt_ref[:, cols] = hot
        local = full_dot(interp, interp * pot_ref[:, cell : cell + 1], TN)
        local = local + stiff_ref[...] * scale_ref[0:1, cell : cell + 1]
        high, mid, low = split3(local)
        for index, part in enumerate((high, mid, low)):
            w_ref[index, :, cols] = lax.dot_general(
                hot, part, NN, preferred_element_type=F32
            ).astype(BF16)
    for first in range(0, ext, PAD):
        block = slice(first, first + PAD)
        hot = gt_ref[...]
        high, mid, low = (
            lax.dot_general(w_ref[index, block, :], hot, NT, preferred_element_type=F32)
            for index in range(3)
        )
        a_ref[block, :] = (low + mid) + high


def filter_kernel(
    ndom,
    fits,
    node_dev,
    spec_ref,
    v_ref,
    a_ref,
    bottom_ref,
    mass_ref,
    occ_ref,
    vall_out,
    gram_out,
    occ_out,
    cur,
    prev,
    vb,
    rb,
    gslot,
    rslot,
    kp,
    vall,
    occs,
    gp,
    rs,
    gall,
    fsend,
    frecv,
    rsend,
    rrecv,
    ksem,
    psend,
    precv,
    ssend,
    srecv,
    gsend,
    grecv,
):
    d = lax.axis_index("dom")
    o = lax.axis_index("orb")
    other = 1 - o
    own = v_ref.shape[0]
    nodes = cur.shape[1]
    has_prev = d > 0
    has_next = d < ndom - 1
    before = lax.rem(d + ndom - 1, ndom)
    after = lax.rem(d + 1, ndom)

    gslot[...] = jnp.zeros_like(gslot)
    rslot[...] = jnp.zeros_like(rslot)
    kp[...] = jnp.zeros_like(kp)

    barrier = pltpu.get_barrier_semaphore()
    pl.semaphore_signal(
        barrier, inc=1, device_id={"dom": d, "orb": other}, device_id_type=MESH
    )
    if fits:

        def greet(k, carry):
            pl.semaphore_signal(
                barrier,
                inc=1,
                device_id={"dom": lax.rem(d + k, ndom), "orb": o},
                device_id_type=MESH,
            )
            return carry

        lax.fori_loop(1, ndom, greet, 0)
        pl.semaphore_wait(barrier, ndom)
    else:
        for ok, peer in ((has_prev, before), (has_next, after)):

            @pl.when(ok)
            def _():
                pl.semaphore_signal(
                    barrier, inc=1, device_id={"dom": peer, "orb": o}, device_id_type=MESH
                )
                pl.semaphore_wait(barrier, 1)

        pl.semaphore_wait(barrier, 1)

    def remote(src, dst, send, recv, dom, orb):
        return pltpu.make_async_remote_copy(
            src_ref=src,
            dst_ref=dst,
            send_sem=send,
            recv_sem=recv,
            device_id={"dom": dom, "orb": orb},
            device_id_type=MESH,
        )

    def face(step):
        return remote(
            vb.at[step], gslot.at[step], fsend.at[step], frecv.at[step], before, o
        )

    def rim(step):
        return remote(rb.at[step], rslot.at[step], rsend.at[step], rrecv.at[step], after, o)

    corner = remote(
        a_ref.at[pl.ds(nodes, PAD), pl.ds(nodes, PAD)], kp, ksem.at[0], ksem.at[1], after, o
    )

    @pl.when(has_next)
    def _():
        corner.start()

    occs[o] = jnp.broadcast_to(occ_ref[...], occs.shape[1:])
    occ_copy = remote(occs.at[o], occs.at[o], psend.at[0], precv.at[0], d, other)
    occ_copy.start()

    halfwidth = (spec_ref[1] - spec_ref[0]) / 2.0
    centre = (spec_ref[1] + spec_ref[0]) / 2.0
    cur[...] = jnp.zeros_like(cur)
    cur[:, :node_dev] = v_ref[...]
    hot = (
        lax.broadcasted_iota(jnp.int32, (nodes, PAD), 0) == bottom_ref[...]
    ).astype(F32).astype(BF16)

    for step in range(DEG):
        value = cur[...]
        edge = pick_dot(value, hot)
        vb[step] = edge

        @pl.when(has_prev)
        def _():
            face(step).start()

        rb[step] = full_dot(value, a_ref[:nodes, nodes:])

        @pl.when(has_next)
        def _():
            rim(step).start()

        total = full_dot(value, a_ref[:nodes, :nodes])
        if step == 0:

            @pl.when(has_prev)
            def _():
                corner.wait_recv()

        extra = full_dot(edge, kp[...])

        @pl.when(has_next)
        def _():
            face(step).wait_recv()

        @pl.when(has_prev)
        def _():
            rim(step).wait_recv()

        total = total + full_dot(gslot[step], a_ref[nodes:, :nodes])
        total = total + pick_dot(extra + rslot[step], hot, NT)
        applied = (total / mass_ref[...] - centre * value) / halfwidth
        if step > 0:
            applied = 2.0 * applied - prev[...]
        prev[...] = value
        cur[...] = applied

    value = cur[...]
    vall[o, :, :nodes] = value
    half = remote(
        vall.at[o, :, pl.ds(0, nodes)],
        vall.at[o, :, pl.ds(0, nodes)],
        psend.at[1],
        precv.at[1],
        d,
        other,
    )
    half.start()
    vb[DEG] = pick_dot(value, hot)

    @pl.when(has_prev)
    def _():
        face(DEG).start()

    weighted = value * mass_ref[...]
    gp[o] = full_dot(weighted, value, NT)
    half.wait_recv()
    gp[other] = full_dot(weighted, vall[other, :, :nodes], NT)

    @pl.when(has_next)
    def _():
        face(DEG).wait_recv()

    vall[o, :, nodes:] = gslot[DEG]
    ghost = remote(
        vall.at[o, :, pl.ds(nodes, PAD)],
        vall.at[o, :, pl.ds(nodes, PAD)],
        psend.at[2],
        precv.at[2],
        d,
        other,
    )
    ghost.start()

    if fits:
        share = own // ndom

        def scatter(k):
            peer = lax.rem(d + k, ndom)
            return remote(
                gp.at[:, pl.ds(pl.multiple_of(peer * share, 8), share), :],
                rs.at[k],
                ssend.at[k],
                srecv.at[k],
                peer,
                o,
            )

        mine = pl.ds(pl.multiple_of(d * share, 8), share)

        def gather(k):
            return remote(
                gall.at[o, :, mine, :],
                gall.at[o, :, mine, :],
                gsend.at[k],
                grecv.at[k],
                lax.rem(d + k, ndom),
                o,
            )

        def arrive(k):
            came = lax.rem(d + ndom - k, ndom)
            spot = pl.ds(pl.multiple_of(came * share, 8), share)
            return remote(
                gall.at[o, :, spot, :],
                gall.at[o, :, spot, :],
                gsend.at[k],
                grecv.at[k],
                came,
                o,
            )

        def run(action):
            lax.fori_loop(1, ndom, lambda k, carry: (action(k), carry)[1], 0)

        run(lambda k: scatter(k).start())
        run(lambda k: scatter(k).wait_recv())
        rs[0] = gp[:, mine, :]
        total = rs[0]
        for k in range(1, ndom):
            total = total + rs[k]
        gall[o, :, mine, :] = total / (ndom * node_dev)
        run(lambda k: gather(k).start())
        run(lambda k: arrive(k).wait_recv())
        swap = remote(gall.at[o], gall.at[o], psend.at[3], precv.at[3], d, other)
        swap.start()
        swap.wait_recv()
        for row in range(2):
            for col in range(2):
                gram_out[row * own : (row + 1) * own, col * own : (col + 1) * own] = gall[
                    row, col
                ]
        run(lambda k: scatter(k).wait_send())
        run(lambda k: gather(k).wait_send())
        swap.wait_send()
    else:
        whole = [vall[0, :, :nodes], vall[1, :, :nodes]]
        for row in range(2):
            for col in range(2):
                gram_out[row * own : (row + 1) * own, col * own : (col + 1) * own] = full_dot(
                    whole[row] * mass_ref[...], whole[col], NT
                )

    ghost.wait_recv()
    occ_copy.wait_recv()
    vall_out[...] = vall[...]
    occ_out[...] = occs[...]
    occ_copy.wait_send()
    half.wait_send()
    ghost.wait_send()
    for step in range(DEG + 1):

        @pl.when(has_prev)
        def _():
            face(step).wait_send()

    for step in range(DEG):

        @pl.when(has_next)
        def _():
            rim(step).wait_send()

    @pl.when(has_next)
    def _():
        corner.wait_send()


def small_inverse(tile, side, size):
    lanes = lax.broadcasted_iota(jnp.int32, tile.shape, 1)
    rows = lax.broadcasted_iota(jnp.int32, tile.shape, 0)
    keep = (lanes >= side * size) & (lanes < (side + 1) * size)
    unit = (lanes - (1 - side) * size == rows).astype(F32)
    work = jnp.where(keep, tile, unit)
    pieces = [work[8 * g : 8 * g + 8] for g in range(size // 8)]
    below = lax.broadcasted_iota(jnp.int32, (8, 1), 0)
    for j in range(size):
        group, row = divmod(j, 8)
        lane = side * size + j
        pivot_row = pieces[group][row : row + 1, :]
        scaled = pivot_row / pivot_row[:, lane : lane + 1]
        for g in range(group, size // 8):
            factor = pieces[g][:, lane : lane + 1]
            if g == group:
                if row == 7:
                    continue
                factor = jnp.where(below > row, factor, 0.0)
            pieces[g] = pieces[g] - factor * scaled
    work = jnp.concatenate(pieces, axis=0)
    diag = jnp.sum(jnp.where(lanes - side * size == rows, work, 0.0), axis=1, keepdims=True)
    work = work * (1.0 / jnp.sqrt(diag))
    return work[:, (1 - side) * size : (2 - side) * size]


def density_kernel(gram_ref, vall_ref, gt_ref, interp_ref, occ_ref, out_ref, w_ref, x_ref):
    orbs = gram_ref.shape[0]
    own = vall_ref.shape[1]
    size = 64
    w_ref[:, :orbs] = gram_ref[...]
    shape = (orbs, orbs)
    w_ref[:, orbs:] = (
        lax.broadcasted_iota(jnp.int32, shape, 0) == lax.broadcasted_iota(jnp.int32, shape, 1)
    ).astype(F32)
    for first in range(0, orbs, size):
        last = first + size
        base = first // LANE * LANE
        tile = w_ref[first:last, base : base + LANE]
        lower = small_inverse(tile, (first - base) // size, size)
        step = full_dot(lower, w_ref[first:last, :])
        x_ref[first:last, :] = step[:, orbs:]
        if last < orbs:
            w_ref[...] = w_ref[...] - full_dot(step[:, :orbs], step, TN)
    inverse = x_ref[...]
    occ = jnp.concatenate([occ_ref[0, 0:1, :own], occ_ref[1, 0:1, :own]], axis=1)
    whole = jnp.concatenate([vall_ref[0], vall_ref[1]], axis=0)
    local = pick_dot(whole, gt_ref[...])
    for cell in range(out_ref.shape[0]):
        quad = full_dot(local[:, cell * LANE : (cell + 1) * LANE], interp_ref[...], NT)
        ortho = full_dot(inverse, quad)
        out_ref[cell : cell + 1, :] = full_dot(occ, ortho * ortho) / orbs


def per_device(
    ndom, block, conn, bottom, cell_scale, potential, mass, stiffness, interp, occupancy, spectrum
):
    own, node_dev = block.shape
    npc, cells = conn.shape
    gauss = interp.shape[0]
    nodes = up(node_dev, PAD)
    ext = nodes + PAD
    orbs = 2 * own
    fits = own % (8 * ndom) == 0
    moved = jnp.where(conn >= node_dev, conn + (nodes - node_dev), conn)
    moved = jnp.pad(moved, ((0, LANE - npc), (0, 0)), constant_values=-1).T
    stiff_pad = jnp.pad(stiffness, ((0, LANE - npc), (0, LANE - npc)))
    interp_pad = jnp.pad(interp, ((0, 0), (0, LANE - npc)))
    bottom_pad = jnp.pad(bottom, (0, PAD - bottom.shape[0]), constant_values=-1)[None, :]
    mass_pad = jnp.pad(mass, (0, nodes - node_dev), constant_values=1.0)[None, :]

    vm = pl.BlockSpec(memory_space=pltpu.VMEM)
    sm = pl.BlockSpec(memory_space=pltpu.SMEM)
    local_params = pltpu.CompilerParams(vmem_limit_bytes=VLIMIT)
    matrix, onehot = pl.pallas_call(
        assemble_kernel,
        name="assemble",
        out_shape=(
            jax.ShapeDtypeStruct((ext, ext), F32),
            jax.ShapeDtypeStruct((ext, cells * LANE), BF16),
        ),
        in_specs=[vm] * 5,
        out_specs=(vm, vm),
        scratch_shapes=[pltpu.VMEM((3, ext, cells * LANE), BF16)],
        compiler_params=local_params,
    )(moved, cell_scale[None, :], potential, stiff_pad, interp_pad)

    dma = pltpu.SemaphoreType.DMA
    peers = ndom if fits else 1
    share = own // ndom if fits else 8
    vall, gram, occ = pl.pallas_call(
        functools.partial(filter_kernel, ndom, fits, node_dev),
        name="filter",
        out_shape=(
            jax.ShapeDtypeStruct((2, own, ext), F32),
            jax.ShapeDtypeStruct((orbs, orbs), F32),
            jax.ShapeDtypeStruct((2, 8, own), F32),
        ),
        in_specs=[sm] + [vm] * 5,
        out_specs=(vm, vm, vm),
        scratch_shapes=[
            pltpu.VMEM((own, nodes), F32),
            pltpu.VMEM((own, nodes), F32),
            pltpu.VMEM((DEG + 1, own, PAD), F32),
            pltpu.VMEM((DEG, own, PAD), F32),
            pltpu.VMEM((DEG + 1, own, PAD), F32),
            pltpu.VMEM((DEG, own, PAD), F32),
            pltpu.VMEM((PAD, PAD), F32),
            pltpu.VMEM((2, own, ext), F32),
            pltpu.VMEM((2, 8, own), F32),
            pltpu.VMEM((2, own, own), F32),
            pltpu.VMEM((peers, 2, share, own), F32),
            pltpu.VMEM((2, 2, own, own), F32),
            dma((DEG + 1,)),
            dma((DEG + 1,)),
            dma((DEG,)),
            dma((DEG,)),
            dma((2,)),
            dma((4,)),
            dma((4,)),
            dma((peers,)),
            dma((peers,)),
            dma((peers,)),
            dma((peers,)),
        ],
        compiler_params=pltpu.CompilerParams(
            collective_id=0, has_side_effects=True, vmem_limit_bytes=VLIMIT
        ),
    )(spectrum, block, matrix, bottom_pad, mass_pad, occupancy[None, :])
    if not fits:
        gram = lax.psum(gram, "dom") / (ndom * node_dev)

    density = pl.pallas_call(
        density_kernel,
        name="density",
        out_shape=jax.ShapeDtypeStruct((cells, gauss), F32),
        in_specs=[vm] * 5,
        out_specs=vm,
        scratch_shapes=[pltpu.VMEM((orbs, 2 * orbs), F32), pltpu.VMEM((orbs, orbs), F32)],
        compiler_params=local_params,
    )(gram, vall, onehot, interp_pad, occ)
    return density.T


def solution(mesh):
    in_specs = (
        P("orb", "dom"),
        P(None, "dom"),
        P("dom"),
        P("dom"),
        P(None, "dom"),
        P("dom"),
        P(),
        P(),
        P("orb"),
        P(),
    )
    out_specs = P(None, "dom")
    return jax.shard_map(
        functools.partial(per_device, mesh.shape["dom"]),
        mesh=mesh,
        in_specs=in_specs,
        out_specs=out_specs,
        check_vma=False,
    )
```

```python
import functools

import jax
import jax.numpy as jnp
from jax import lax
from jax.experimental import pallas as pl
from jax.experimental.pallas import tpu as pltpu
from jax.sharding import PartitionSpec as P

DEG = 3
LANE = 128
PAD = 256
HI = lax.Precision.HIGHEST
MESH = pl.DeviceIdType.MESH
F32 = jnp.float32
BF16 = jnp.bfloat16
NN = (((1,), (0,)), ((), ()))
NT = (((1,), (1,)), ((), ()))
TN = (((0,), (0,)), ((), ()))
VLIMIT = 48 * 1024 * 1024


def up(value, unit):
    return -(-value // unit) * unit


def full_dot(left, right, dims=NN):
    return lax.dot_general(left, right, dims, precision=HI, preferred_element_type=F32)


def split2(value):
    high = value.astype(BF16)
    return high, (value - high.astype(F32)).astype(BF16)


def part_dot(left, right, dims=NN):
    return lax.dot_general(left, right, dims, preferred_element_type=F32)


def dot3(left, right, dims=NN):
    high, low = left
    main, rest = right
    return (part_dot(low, main, dims) + part_dot(high, rest, dims)) + part_dot(high, main, dims)


def pick_dot(parts, onehot, dims=NN):
    high, low = parts
    return part_dot(low, onehot, dims) + part_dot(high, onehot, dims)


def assemble_kernel(
    conn_ref, scale_ref, pot_ref, stiff_ref, interp_ref, ah_ref, al_ref, gt_ref, w_ref, k_ref, b_ref
):
    ext = ah_ref.shape[0]
    cells = conn_ref.shape[0]
    npc = stiff_ref.shape[0]
    k_ref[...] = jnp.zeros_like(k_ref)
    k_ref[:npc, :npc] = stiff_ref[...]
    b_ref[...] = jnp.zeros_like(b_ref)
    b_ref[:, :npc] = interp_ref[...]
    interp = b_ref[...]
    parts = split2(interp)
    rows = lax.broadcasted_iota(jnp.int32, (ext, LANE), 0)
    for cell in range(cells):
        cols = slice(cell * LANE, (cell + 1) * LANE)
        hot = (rows == conn_ref[cell : cell + 1, :]).astype(F32).astype(BF16)
        gt_ref[:, cols] = hot
        local = dot3(parts, split2(interp * pot_ref[:, cell : cell + 1]), TN)
        local = local + k_ref[...] * scale_ref[0:1, cell : cell + 1]
        both = part_dot(hot, jnp.concatenate(split2(local), axis=1)).astype(BF16)
        w_ref[0, :, cols] = both[:, :LANE]
        w_ref[1, :, cols] = both[:, LANE:]
    for first in range(0, ext, PAD):
        for second in range(first, ext, PAD):
            here, there = slice(first, first + PAD), slice(second, second + PAD)
            hot = gt_ref[there, :]
            block = part_dot(w_ref[1, here, :], hot, NT) + part_dot(w_ref[0, here, :], hot, NT)
            ah_ref[here, there], al_ref[here, there] = split2(block)
            if second > first:
                ah_ref[there, here], al_ref[there, here] = split2(block.T)


def filter_kernel(
    ndom,
    fits,
    node_dev,
    spec_ref,
    v_ref,
    ah_ref,
    al_ref,
    bottom_ref,
    mass_ref,
    occ_ref,
    vall_out,
    gram_out,
    occ_out,
    cur,
    prev,
    vb,
    rb,
    gslot,
    rslot,
    kp,
    edge_block,
    mass_row,
    bottom_row,
    vall,
    occs,
    gp,
    rs,
    gall,
    fsend,
    frecv,
    rsend,
    rrecv,
    ksem,
    psend,
    precv,
    ssend,
    srecv,
    gsend,
    grecv,
):
    d = lax.axis_index("dom")
    o = lax.axis_index("orb")
    other = 1 - o
    own = v_ref.shape[0]
    nodes = cur.shape[1]
    has_prev = d > 0
    has_next = d < ndom - 1
    before = lax.rem(d + ndom - 1, ndom)
    after = lax.rem(d + 1, ndom)

    gslot[...] = jnp.zeros_like(gslot)
    rslot[...] = jnp.zeros_like(rslot)
    kp[...] = jnp.zeros_like(kp)
    edge_block[...] = ah_ref[nodes:, nodes:].astype(F32) + al_ref[nodes:, nodes:].astype(F32)

    barrier = pltpu.get_barrier_semaphore()
    pl.semaphore_signal(
        barrier, inc=1, device_id={"dom": d, "orb": other}, device_id_type=MESH
    )
    if fits:

        def greet(k, carry):
            pl.semaphore_signal(
                barrier,
                inc=1,
                device_id={"dom": lax.rem(d + k, ndom), "orb": o},
                device_id_type=MESH,
            )
            return carry

        lax.fori_loop(1, ndom, greet, 0)
        pl.semaphore_wait(barrier, ndom)
    else:
        for ok, peer in ((has_prev, before), (has_next, after)):

            @pl.when(ok)
            def _():
                pl.semaphore_signal(
                    barrier, inc=1, device_id={"dom": peer, "orb": o}, device_id_type=MESH
                )
                pl.semaphore_wait(barrier, 1)

        pl.semaphore_wait(barrier, 1)

    def remote(src, dst, send, recv, dom, orb):
        return pltpu.make_async_remote_copy(
            src_ref=src,
            dst_ref=dst,
            send_sem=send,
            recv_sem=recv,
            device_id={"dom": dom, "orb": orb},
            device_id_type=MESH,
        )

    def face(step):
        return remote(
            vb.at[step], gslot.at[step], fsend.at[step], frecv.at[step], before, o
        )

    def rim(step):
        return remote(rb.at[step], rslot.at[step], rsend.at[step], rrecv.at[step], after, o)

    corner = remote(
        edge_block, kp, ksem.at[0], ksem.at[1], after, o
    )

    @pl.when(has_next)
    def _():
        corner.start()

    occs[o] = jnp.broadcast_to(occ_ref[...], occs.shape[1:])
    occ_copy = remote(occs.at[o], occs.at[o], psend.at[0], precv.at[0], d, other)
    occ_copy.start()

    halfwidth = (spec_ref[1] - spec_ref[0]) / 2.0
    centre = (spec_ref[1] + spec_ref[0]) / 2.0
    cur[...] = jnp.zeros_like(cur)
    cur[:, :node_dev] = v_ref[...]
    mass_row[...] = jnp.ones_like(mass_row)
    mass_row[:, :node_dev] = mass_ref[...]
    bottom_row[...] = jnp.full_like(bottom_row, -1)
    bottom_row[:, : bottom_ref.shape[1]] = bottom_ref[...]
    mass = mass_row[...]
    over_mass = 1.0 / (mass * halfwidth)
    shift = centre / halfwidth
    hot = (
        lax.broadcasted_iota(jnp.int32, (nodes, PAD), 0) == bottom_row[...]
    ).astype(F32).astype(BF16)

    for step in range(DEG):
        value = cur[...]
        parts = split2(value)
        edge = pick_dot(parts, hot)
        vb[step] = edge

        @pl.when(has_prev)
        def _():
            face(step).start()

        rb[step] = dot3(parts, (ah_ref[:nodes, nodes:], al_ref[:nodes, nodes:]))

        @pl.when(has_next)
        def _():
            rim(step).start()

        total = dot3(parts, (ah_ref[:nodes, :nodes], al_ref[:nodes, :nodes]))
        if step == 0:

            @pl.when(has_prev)
            def _():
                corner.wait_recv()

        extra = dot3(split2(edge), split2(kp[...]))

        @pl.when(has_next)
        def _():
            face(step).wait_recv()

        @pl.when(has_prev)
        def _():
            rim(step).wait_recv()

        total = total + dot3(
            split2(gslot[step]), (ah_ref[nodes:, :nodes], al_ref[nodes:, :nodes])
        )
        total = total + pick_dot(split2(extra + rslot[step]), hot, NT)
        applied = total * over_mass - shift * value
        if step > 0:
            applied = 2.0 * applied - prev[...]
        prev[...] = value
        cur[...] = applied

    value = cur[...]
    vall[o, :, :nodes] = value
    half = remote(
        vall.at[o, :, pl.ds(0, nodes)],
        vall.at[o, :, pl.ds(0, nodes)],
        psend.at[1],
        precv.at[1],
        d,
        other,
    )
    half.start()
    vb[DEG] = pick_dot(split2(value), hot)

    @pl.when(has_prev)
    def _():
        face(DEG).start()

    weighted = value * mass
    gp[o] = full_dot(weighted, value, NT)
    half.wait_recv()
    gp[other] = full_dot(weighted, vall[other, :, :nodes], NT)

    @pl.when(has_next)
    def _():
        face(DEG).wait_recv()

    vall[o, :, nodes:] = gslot[DEG]
    ghost = remote(
        vall.at[o, :, pl.ds(nodes, PAD)],
        vall.at[o, :, pl.ds(nodes, PAD)],
        psend.at[2],
        precv.at[2],
        d,
        other,
    )
    ghost.start()

    if fits:
        share = own // ndom

        def scatter(k):
            peer = lax.rem(d + k, ndom)
            return remote(
                gp.at[:, pl.ds(pl.multiple_of(peer * share, 8), share), :],
                rs.at[k],
                ssend.at[k],
                srecv.at[k],
                peer,
                o,
            )

        mine = pl.ds(pl.multiple_of(d * share, 8), share)

        def gather(k):
            return remote(
                gall.at[o, :, mine, :],
                gall.at[o, :, mine, :],
                gsend.at[k],
                grecv.at[k],
                lax.rem(d + k, ndom),
                o,
            )

        def arrive(k):
            came = lax.rem(d + ndom - k, ndom)
            spot = pl.ds(pl.multiple_of(came * share, 8), share)
            return remote(
                gall.at[o, :, spot, :],
                gall.at[o, :, spot, :],
                gsend.at[k],
                grecv.at[k],
                came,
                o,
            )

        def run(action):
            lax.fori_loop(1, ndom, lambda k, carry: (action(k), carry)[1], 0)

        run(lambda k: scatter(k).start())
        run(lambda k: scatter(k).wait_recv())
        rs[0] = gp[:, mine, :]
        total = rs[0]
        for k in range(1, ndom):
            total = total + rs[k]
        gall[o, :, mine, :] = total / (ndom * node_dev)
        run(lambda k: gather(k).start())
        run(lambda k: arrive(k).wait_recv())
        swap = remote(gall.at[o], gall.at[o], psend.at[3], precv.at[3], d, other)
        swap.start()
        swap.wait_recv()
        for row in range(2):
            for col in range(2):
                gram_out[row * own : (row + 1) * own, col * own : (col + 1) * own] = gall[
                    row, col
                ]
        run(lambda k: scatter(k).wait_send())
        run(lambda k: gather(k).wait_send())
        swap.wait_send()
    else:
        whole = [vall[0, :, :nodes], vall[1, :, :nodes]]
        for row in range(2):
            for col in range(2):
                gram_out[row * own : (row + 1) * own, col * own : (col + 1) * own] = full_dot(
                    whole[row] * mass, whole[col], NT
                )

    ghost.wait_recv()
    occ_copy.wait_recv()
    vall_out[...] = vall[...]
    occ_out[...] = occs[...]
    occ_copy.wait_send()
    half.wait_send()
    ghost.wait_send()
    for step in range(DEG + 1):

        @pl.when(has_prev)
        def _():
            face(step).wait_send()

    for step in range(DEG):

        @pl.when(has_next)
        def _():
            rim(step).wait_send()

    @pl.when(has_next)
    def _():
        corner.wait_send()


def small_inverse(tile, side, size, filler):
    lanes = lax.broadcasted_iota(jnp.int32, tile.shape, 1)
    rows = lax.broadcasted_iota(jnp.int32, tile.shape, 0)
    keep = (lanes >= side * size) & (lanes < (side + 1) * size)
    unit = (lanes - (1 - side) * size == rows).astype(F32)
    work = jnp.where(keep, tile, unit)
    groups = size // 8
    pieces = [work[8 * g : 8 * g + 8] for g in range(groups)]
    below = lax.broadcasted_iota(jnp.int32, (8, LANE), 0)
    panel = 4
    full = (8, LANE)
    for start in range(0, size, panel):
        top, row = divmod(start, 8)
        lane = side * size + start
        head = [pieces[top][row + a : row + a + 1, :] for a in range(panel)]
        line = [jnp.broadcast_to(value, full) for value in head]
        pivot = [
            [
                jnp.broadcast_to(head[a][:, lane + b : lane + b + 1], full) if b >= a else None
                for b in range(panel)
            ]
            for a in range(panel)
        ]
        column = [
            [
                jnp.broadcast_to(pieces[g][:, lane + b : lane + b + 1], full)
                for b in range(panel)
            ]
            for g in range(top, groups)
        ]
        for a in range(panel):
            over = 1.0 / pivot[a][a]
            for g in range(top, groups):
                if g == top and row + a == 7:
                    continue
                terms = column[g - top]
                factor = terms[a] * over
                if g == top:
                    factor = jnp.where(below > row + a, factor, 0.0)
                pieces[g] = pieces[g] - factor * line[a]
                for b in range(a + 1, panel):
                    terms[b] = terms[b] - factor * pivot[a][b]
            for b in range(a + 1, panel):
                factor = pivot[a][b] * over
                line[b] = line[b] - factor * line[a]
                for c in range(b, panel):
                    pivot[b][c] = pivot[b][c] - factor * pivot[a][c]
        if start // panel % 3 == 1:
            next(filler, None)
    work = jnp.concatenate(pieces, axis=0)
    diag = jnp.sum(jnp.where(lanes - side * size == rows, work, 0.0), axis=1, keepdims=True)
    work = work * (1.0 / jnp.sqrt(diag))
    return work[:, (1 - side) * size : (2 - side) * size]


def density_kernel(
    gram_ref, vall_ref, gt_ref, interp_ref, occ_ref, out_ref, w_ref, x_ref, v_ref, q_ref, b_ref
):
    orbs = gram_ref.shape[0]
    own = vall_ref.shape[1]
    cells = out_ref.shape[0]
    gauss, npc = interp_ref.shape
    size = 64
    w_ref[:, :orbs] = gram_ref[...]
    shape = (orbs, orbs)
    eye = lax.broadcasted_iota(jnp.int32, shape, 0) == lax.broadcasted_iota(jnp.int32, shape, 1)
    w_ref[:, orbs:] = eye.astype(F32)
    b_ref[...] = jnp.zeros_like(b_ref)
    b_ref[:, :npc] = interp_ref[...]
    basis = split2(b_ref[...])
    for half in range(2):
        part = slice(half * own, (half + 1) * own)
        v_ref[0, part, :], v_ref[1, part, :] = split2(vall_ref[half])

    def quadrature():
        for cell in range(cells):
            local = pick_dot(
                (v_ref[0], v_ref[1]), gt_ref[:, cell * LANE : (cell + 1) * LANE]
            )
            yield
            q_ref[0, cell], q_ref[1, cell] = split2(dot3(split2(local), basis, NT))
            yield

    filler = quadrature()
    for first in range(0, orbs, size):
        last = first + size
        base = first // LANE * LANE
        tile = w_ref[first:last, base : base + LANE]
        lower = small_inverse(tile, (first - base) // size, size, filler)
        step = full_dot(lower, w_ref[first:last, :])
        x_ref[first:last, :] = step[:, orbs:]
        if last < orbs:
            w_ref[last:, :] = w_ref[last:, :] - full_dot(step[:, last:orbs], step, TN)
    for _ in filler:
        pass
    inverse = split2(x_ref[...])
    occ = jnp.concatenate([occ_ref[0, 0:1, :own], occ_ref[1, 0:1, :own]], axis=1)
    weight = jnp.sum(jnp.where(eye, occ, 0.0), axis=1, keepdims=True) / orbs
    for cell in range(cells):
        ortho = dot3(inverse, (q_ref[0, cell], q_ref[1, cell]))
        out_ref[cell : cell + 1, :] = jnp.sum(weight * (ortho * ortho), axis=0, keepdims=True)


def per_device(
    ndom, block, conn, bottom, cell_scale, potential, mass, stiffness, interp, occupancy, spectrum
):
    own, node_dev = block.shape
    npc, cells = conn.shape
    gauss = interp.shape[0]
    nodes = up(node_dev, PAD)
    ext = nodes + PAD
    orbs = 2 * own
    fits = own % (8 * ndom) == 0
    moved = jnp.where(conn >= node_dev, conn + (nodes - node_dev), conn)
    moved = jnp.pad(moved, ((0, LANE - npc), (0, 0)), constant_values=-1).T
    vm = pl.BlockSpec(memory_space=pltpu.VMEM)
    sm = pl.BlockSpec(memory_space=pltpu.SMEM)
    local_params = pltpu.CompilerParams(vmem_limit_bytes=VLIMIT)
    high, low, onehot = pl.pallas_call(
        assemble_kernel,
        name="assemble",
        out_shape=(
            jax.ShapeDtypeStruct((ext, ext), BF16),
            jax.ShapeDtypeStruct((ext, ext), BF16),
            jax.ShapeDtypeStruct((ext, cells * LANE), BF16),
        ),
        in_specs=[vm] * 5,
        out_specs=(vm, vm, vm),
        scratch_shapes=[
            pltpu.VMEM((2, ext, cells * LANE), BF16),
            pltpu.VMEM((LANE, LANE), F32),
            pltpu.VMEM((gauss, LANE), F32),
        ],
        compiler_params=local_params,
    )(moved, cell_scale[None, :], potential, stiffness, interp)

    dma = pltpu.SemaphoreType.DMA
    peers = ndom if fits else 1
    share = own // ndom if fits else 8
    vall, gram, occ = pl.pallas_call(
        functools.partial(filter_kernel, ndom, fits, node_dev),
        name="filter",
        out_shape=(
            jax.ShapeDtypeStruct((2, own, ext), F32),
            jax.ShapeDtypeStruct((orbs, orbs), F32),
            jax.ShapeDtypeStruct((2, 8, own), F32),
        ),
        in_specs=[sm] + [vm] * 6,
        out_specs=(vm, vm, vm),
        scratch_shapes=[
            pltpu.VMEM((own, nodes), F32),
            pltpu.VMEM((own, nodes), F32),
            pltpu.VMEM((DEG + 1, own, PAD), F32),
            pltpu.VMEM((DEG, own, PAD), F32),
            pltpu.VMEM((DEG + 1, own, PAD), F32),
            pltpu.VMEM((DEG, own, PAD), F32),
            pltpu.VMEM((PAD, PAD), F32),
            pltpu.VMEM((PAD, PAD), F32),
            pltpu.VMEM((1, nodes), F32),
            pltpu.VMEM((1, PAD), jnp.int32),
            pltpu.VMEM((2, own, ext), F32),
            pltpu.VMEM((2, 8, own), F32),
            pltpu.VMEM((2, own, own), F32),
            pltpu.VMEM((peers, 2, share, own), F32),
            pltpu.VMEM((2, 2, own, own), F32),
            dma((DEG + 1,)),
            dma((DEG + 1,)),
            dma((DEG,)),
            dma((DEG,)),
            dma((2,)),
            dma((4,)),
            dma((4,)),
            dma((peers,)),
            dma((peers,)),
            dma((peers,)),
            dma((peers,)),
        ],
        compiler_params=pltpu.CompilerParams(
            collective_id=0, has_side_effects=True, vmem_limit_bytes=VLIMIT
        ),
    )(spectrum, block, high, low, bottom[None, :], mass[None, :], occupancy[None, :])
    if not fits:
        gram = lax.psum(gram, "dom") / (ndom * node_dev)

    density = pl.pallas_call(
        density_kernel,
        name="density",
        out_shape=jax.ShapeDtypeStruct((cells, gauss), F32),
        in_specs=[vm] * 5,
        out_specs=vm,
        scratch_shapes=[
            pltpu.VMEM((orbs, 2 * orbs), F32),
            pltpu.VMEM((orbs, orbs), F32),
            pltpu.VMEM((2, orbs, ext), BF16),
            pltpu.VMEM((2, cells, orbs, gauss), BF16),
            pltpu.VMEM((gauss, LANE), F32),
        ],
        compiler_params=local_params,
    )(gram, vall, onehot, interp, occ)
    return density.T


def solution(mesh):
    in_specs = (
        P("orb", "dom"),
        P(None, "dom"),
        P("dom"),
        P("dom"),
        P(None, "dom"),
        P("dom"),
        P(),
        P(),
        P("orb"),
        P(),
    )
    out_specs = P(None, "dom")
    return jax.shard_map(
        functools.partial(per_device, mesh.shape["dom"]),
        mesh=mesh,
        in_specs=in_specs,
        out_specs=out_specs,
        check_vma=False,
    )
```

```python
import functools

import jax
import jax.numpy as jnp
from jax import lax
from jax.experimental import pallas as pl
from jax.experimental.pallas import tpu as pltpu
from jax.sharding import PartitionSpec as P

DEG = 3
LANE = 128
PAD = 256
HI = lax.Precision.HIGHEST
MESH = pl.DeviceIdType.MESH
F32 = jnp.float32
BF16 = jnp.bfloat16
NN = (((1,), (0,)), ((), ()))
NT = (((1,), (1,)), ((), ()))
TN = (((0,), (0,)), ((), ()))
TT = (((0,), (1,)), ((), ()))
VLIMIT = 48 * 1024 * 1024


def up(value, unit):
    return -(-value // unit) * unit


def full_dot(left, right, dims=NN):
    return lax.dot_general(left, right, dims, precision=HI, preferred_element_type=F32)


def split2(value):
    high = value.astype(BF16)
    return high, (value - high.astype(F32)).astype(BF16)


def part_dot(left, right, dims=NN):
    return lax.dot_general(left, right, dims, preferred_element_type=F32)


def dot3(left, right, dims=NN):
    high, low = left
    main, rest = right
    return (part_dot(low, main, dims) + part_dot(high, rest, dims)) + part_dot(high, main, dims)


def pick_dot(parts, onehot, dims=NN):
    high, low = parts
    return part_dot(low, onehot, dims) + part_dot(high, onehot, dims)


def assemble(
    conn_ref, scale_ref, pot_ref, stiff_ref, interp_ref, ah_ref, al_ref, corner_ref, gt_ref, w_ref, k_ref, b_ref
):
    ext = ah_ref.shape[0]
    cells = conn_ref.shape[0]
    npc = stiff_ref.shape[0]
    k_ref[...] = jnp.zeros_like(k_ref)
    k_ref[:npc, :npc] = stiff_ref[...]
    b_ref[...] = jnp.zeros_like(b_ref)
    b_ref[:, :npc] = interp_ref[...]
    interp = b_ref[...]
    parts = split2(interp)
    rows = lax.broadcasted_iota(jnp.int32, (ext, LANE), 0)
    for cell in range(cells):
        cols = slice(cell * LANE, (cell + 1) * LANE)
        hot = (rows == conn_ref[cell : cell + 1, :]).astype(F32).astype(BF16)
        gt_ref[:, cols] = hot
        local = dot3(parts, split2(interp * pot_ref[:, cell : cell + 1]), TN)
        local = local + k_ref[...] * scale_ref[0:1, cell : cell + 1]
        both = part_dot(hot, jnp.concatenate(split2(local), axis=1)).astype(BF16)
        w_ref[0, :, cols] = both[:, :LANE]
        w_ref[1, :, cols] = both[:, LANE:]
    for first in range(0, ext, PAD):
        for second in range(first, ext, PAD):
            here, there = slice(first, first + PAD), slice(second, second + PAD)
            hot = gt_ref[there, :]
            block = part_dot(w_ref[1, here, :], hot, NT) + part_dot(w_ref[0, here, :], hot, NT)
            ah_ref[here, there], al_ref[here, there] = split2(block)
            if second > first:
                ah_ref[there, here], al_ref[there, here] = split2(block.T)
            if first == ext - PAD:
                corner_ref[...] = block


def filter_kernel(ndom, fits, node_dev, rows, *refs):
    spec_ref, v_ref, conn_ref, scale_ref, pot_ref, stiff_ref, interp_ref = refs[:7]
    bottom_ref, mass_ref, occ_ref = refs[7:10]
    outs = 1 if fits else 3
    outputs = refs[10 : 10 + outs]
    scratch = refs[10 + outs :]
    ah_ref, al_ref, edge_block, gt_ref, w_ref, k_ref, b_ref = scratch[:7]
    cur, prev, vb, rb, gslot, rslot, kp, mass_row, bottom_row = scratch[7:16]
    vall, ghosts, occs, gp, rs, gall, vp, qp, work, inverse_ref = scratch[16:26]
    fsend, frecv, rsend, rrecv, ksem, psend, precv, ssend, srecv, gsend, grecv = scratch[26:]
    d = lax.axis_index("dom")
    o = lax.axis_index("orb")
    other = 1 - o
    own = v_ref.shape[0]
    nodes = cur.shape[1]
    cells = conn_ref.shape[0]
    has_prev = d > 0
    has_next = d < ndom - 1
    before = lax.rem(d + ndom - 1, ndom)
    after = lax.rem(d + 1, ndom)

    gslot[...] = jnp.zeros_like(gslot)
    rslot[...] = jnp.zeros_like(rslot)
    kp[...] = jnp.zeros_like(kp)
    ghosts[...] = jnp.zeros_like(ghosts)

    barrier = pltpu.get_barrier_semaphore()
    pl.semaphore_signal(
        barrier, inc=1, device_id={"dom": d, "orb": other}, device_id_type=MESH
    )
    if fits:

        def greet(k, carry):
            pl.semaphore_signal(
                barrier,
                inc=1,
                device_id={"dom": lax.rem(d + k, ndom), "orb": o},
                device_id_type=MESH,
            )
            return carry

        lax.fori_loop(1, ndom, greet, 0)
    else:
        for ok, peer in ((has_prev, before), (has_next, after)):

            @pl.when(ok)
            def _():
                pl.semaphore_signal(
                    barrier, inc=1, device_id={"dom": peer, "orb": o}, device_id_type=MESH
                )

    assemble(
        conn_ref, scale_ref, pot_ref, stiff_ref, interp_ref, ah_ref, al_ref, edge_block, gt_ref, w_ref, k_ref, b_ref
    )
    halfwidth = (spec_ref[1] - spec_ref[0]) / 2.0
    centre = (spec_ref[1] + spec_ref[0]) / 2.0
    cur[...] = jnp.zeros_like(cur)
    cur[:, :node_dev] = v_ref[...]
    mass_row[...] = jnp.ones_like(mass_row)
    mass_row[:, :node_dev] = mass_ref[...]
    bottom_row[...] = jnp.full_like(bottom_row, -1)
    bottom_row[:, : bottom_ref.shape[1]] = bottom_ref[...]
    occs[o] = jnp.broadcast_to(occ_ref[...], occs.shape[1:])
    mass = mass_row[...]
    over_mass = 1.0 / (mass * halfwidth)
    shift = centre / halfwidth
    hot = (
        lax.broadcasted_iota(jnp.int32, (nodes, PAD), 0) == bottom_row[...]
    ).astype(F32).astype(BF16)

    if fits:
        pl.semaphore_wait(barrier, ndom)
    else:
        for ok in (has_prev, has_next):

            @pl.when(ok)
            def _():
                pl.semaphore_wait(barrier, 1)

        pl.semaphore_wait(barrier, 1)

    def remote(src, dst, send, recv, dom, orb):
        return pltpu.make_async_remote_copy(
            src_ref=src,
            dst_ref=dst,
            send_sem=send,
            recv_sem=recv,
            device_id={"dom": dom, "orb": orb},
            device_id_type=MESH,
        )

    some = pl.ds(0, rows)

    def face(step):
        return remote(
            vb.at[step, some], gslot.at[step, some], fsend.at[step], frecv.at[step], before, o
        )

    def rim(step):
        return remote(
            rb.at[step, some], rslot.at[step, some], rsend.at[step], rrecv.at[step], after, o
        )

    corner = remote(edge_block.at[some], kp.at[some], ksem.at[0], ksem.at[1], after, o)

    for step in range(DEG):
        value = cur[...]
        parts = split2(value)
        edge = part_dot(hot, parts[1], TT) + part_dot(hot, parts[0], TT)
        vb[step] = edge

        @pl.when(has_prev)
        def _():
            face(step).start()

        rb[step] = dot3((ah_ref[nodes:, :nodes], al_ref[nodes:, :nodes]), parts, NT)

        @pl.when(has_next)
        def _():
            rim(step).start()

        if step == 0:

            @pl.when(has_next)
            def _():
                corner.start()

            occ_copy = remote(occs.at[o], occs.at[o], psend.at[0], precv.at[0], d, other)
            occ_copy.start()

        total = dot3(parts, (ah_ref[:nodes, :nodes], al_ref[:nodes, :nodes]))
        if step == 0:

            @pl.when(has_prev)
            def _():
                corner.wait_recv()

        extra = dot3(split2(kp[...]), split2(edge))

        @pl.when(has_next)
        def _():
            face(step).wait_recv()

        total = total + dot3(
            split2(gslot[step]), (ah_ref[nodes:, :nodes], al_ref[nodes:, :nodes]), TN
        )

        @pl.when(has_prev)
        def _():
            rim(step).wait_recv()

        total = total + pick_dot(split2(extra + rslot[step]), hot, TT)
        applied = total * over_mass - shift * value
        if step > 0:
            applied = 2.0 * applied - prev[...]
        prev[...] = value
        cur[...] = applied

    value = cur[...]
    vall[o] = value
    half = remote(vall.at[o], vall.at[o], psend.at[1], precv.at[1], d, other)
    half.start()
    parts = split2(value)
    vb[DEG] = part_dot(hot, parts[1], TT) + part_dot(hot, parts[0], TT)

    @pl.when(has_prev)
    def _():
        face(DEG).start()

    weighted = value * mass
    gp[o] = full_dot(weighted, value, NT)
    half.wait_recv()
    gp[other] = full_dot(weighted, vall[other], NT)

    def run(action):
        lax.fori_loop(1, ndom, lambda k, carry: (action(k), carry)[1], 0)

    if fits:
        share = own // ndom
        mine = pl.ds(pl.multiple_of(d * share, 8), share)

        def scatter(k):
            peer = lax.rem(d + k, ndom)
            return remote(
                gp.at[:, pl.ds(pl.multiple_of(peer * share, 8), share), :],
                rs.at[k],
                ssend.at[k],
                srecv.at[k],
                peer,
                o,
            )

        def gather(k):
            return remote(
                gall.at[o, :, mine, :],
                gall.at[o, :, mine, :],
                gsend.at[k],
                grecv.at[k],
                lax.rem(d + k, ndom),
                o,
            )

        def arrive(k):
            came = lax.rem(d + ndom - k, ndom)
            spot = pl.ds(pl.multiple_of(came * share, 8), share)
            return remote(
                gall.at[o, :, spot, :],
                gall.at[o, :, spot, :],
                gsend.at[k],
                grecv.at[k],
                came,
                o,
            )

        run(lambda k: scatter(k).start())

    @pl.when(has_next)
    def _():
        face(DEG).wait_recv()

    ghosts[o] = gslot[DEG]
    ghost = remote(
        ghosts.at[o, some], ghosts.at[o, some], psend.at[2], precv.at[2], d, other
    )
    ghost.start()
    for orb in range(2):
        part = slice(orb * own, (orb + 1) * own)
        vp[0, part, :], vp[1, part, :] = split2(vall[orb])
    ghost.wait_recv()
    far = split2(jnp.concatenate([ghosts[0], ghosts[1]], axis=1))
    basis = split2(b_ref[...])

    def quadrature(first, last):
        for cell in range(first, last):
            cols = slice(cell * LANE, (cell + 1) * LANE)
            local = pick_dot((vp[0], vp[1]), gt_ref[:nodes, cols])
            local = local + pick_dot(far, gt_ref[nodes:, cols], TN)
            qp[0, cell], qp[1, cell] = split2(dot3(split2(local), basis, NT))

    cut = cells // 2
    quadrature(0, cut)
    if fits:
        run(lambda k: scatter(k).wait_recv())
        rs[0] = gp[:, mine, :]
        total = rs[0]
        for k in range(1, ndom):
            total = total + rs[k]
        gall[o, :, mine, :] = total / (ndom * node_dev)
        run(lambda k: gather(k).start())
    quadrature(cut, cells)
    occ_copy.wait_recv()
    if fits:
        run(lambda k: arrive(k).wait_recv())
        swap = remote(gall.at[o], gall.at[o], psend.at[3], precv.at[3], d, other)
        swap.start()
        swap.wait_recv()
        for row in range(2):
            for col in range(2):
                work[row * own : (row + 1) * own, col * own : (col + 1) * own] = gall[row, col]
        finish(work, qp, occs, outputs[0], inverse_ref)
        run(lambda k: scatter(k).wait_send())
        run(lambda k: gather(k).wait_send())
        swap.wait_send()
    else:
        gram_out, q_out, occ_out = outputs
        for row in range(2):
            for col in range(2):
                gram_out[row * own : (row + 1) * own, col * own : (col + 1) * own] = full_dot(
                    vall[row] * mass, vall[col], NT
                )
        q_out[...] = qp[...]
        occ_out[...] = occs[...]

    occ_copy.wait_send()
    half.wait_send()
    ghost.wait_send()
    for step in range(DEG + 1):

        @pl.when(has_prev)
        def _():
            face(step).wait_send()

    for step in range(DEG):

        @pl.when(has_next)
        def _():
            rim(step).wait_send()

    @pl.when(has_next)
    def _():
        corner.wait_send()


def small_inverse(tile, side, size):
    lanes = lax.broadcasted_iota(jnp.int32, tile.shape, 1)
    rows = lax.broadcasted_iota(jnp.int32, tile.shape, 0)
    keep = (lanes >= side * size) & (lanes < (side + 1) * size)
    unit = (lanes - (1 - side) * size == rows).astype(F32)
    work = jnp.where(keep, tile, unit)
    groups = size // 8
    pieces = [work[8 * g : 8 * g + 8] for g in range(groups)]
    below = lax.broadcasted_iota(jnp.int32, (8, LANE), 0)
    panel = 4
    full = (8, LANE)
    for start in range(0, size, panel):
        top, row = divmod(start, 8)
        lane = side * size + start
        head = [pieces[top][row + a : row + a + 1, :] for a in range(panel)]
        line = [jnp.broadcast_to(value, full) for value in head]
        pivot = [
            [
                jnp.broadcast_to(head[a][:, lane + b : lane + b + 1], full) if b >= a else None
                for b in range(panel)
            ]
            for a in range(panel)
        ]
        column = [
            [
                jnp.broadcast_to(pieces[g][:, lane + b : lane + b + 1], full)
                for b in range(panel)
            ]
            for g in range(top, groups)
        ]
        for a in range(panel):
            over = 1.0 / pivot[a][a]
            for g in range(top, groups):
                if g == top and row + a == 7:
                    continue
                terms = column[g - top]
                factor = terms[a] * over
                if g == top:
                    factor = jnp.where(below > row + a, factor, 0.0)
                pieces[g] = pieces[g] - factor * line[a]
                for b in range(a + 1, panel):
                    terms[b] = terms[b] - factor * pivot[a][b]
            for b in range(a + 1, panel):
                factor = pivot[a][b] * over
                line[b] = line[b] - factor * line[a]
                for c in range(b, panel):
                    pivot[b][c] = pivot[b][c] - factor * pivot[a][c]
    work = jnp.concatenate(pieces, axis=0)
    diag = jnp.sum(jnp.where(lanes - side * size == rows, work, 0.0), axis=1, keepdims=True)
    work = work * (1.0 / jnp.sqrt(diag))
    return work[:, (1 - side) * size : (2 - side) * size]


def finish(w_ref, q_ref, occ_ref, out_ref, x_ref):
    orbs = x_ref.shape[0]
    own = occ_ref.shape[2]
    size = 64
    shape = (orbs, orbs)
    eye = lax.broadcasted_iota(jnp.int32, shape, 0) == lax.broadcasted_iota(jnp.int32, shape, 1)
    w_ref[:, orbs:] = eye.astype(F32)
    for first in range(0, orbs, size):
        last = first + size
        base = first // LANE * LANE
        tile = w_ref[first:last, base : base + LANE]
        lower = small_inverse(tile, (first - base) // size, size)
        step = full_dot(lower, w_ref[first:last, :])
        x_ref[first:last, :] = step[:, orbs:]
        if last < orbs:
            w_ref[last:, :] = w_ref[last:, :] - full_dot(step[:, last:orbs], step, TN)
    inverse = split2(x_ref[...])
    occ = jnp.concatenate([occ_ref[0, 0:1, :own], occ_ref[1, 0:1, :own]], axis=1)
    weight = jnp.sum(jnp.where(eye, occ, 0.0), axis=1, keepdims=True) / orbs
    for cell in range(out_ref.shape[0]):
        ortho = dot3(inverse, (q_ref[0, cell], q_ref[1, cell]))
        out_ref[cell : cell + 1, :] = jnp.sum(weight * (ortho * ortho), axis=0, keepdims=True)


def density_kernel(gram_ref, q_ref, occ_ref, out_ref, w_ref, x_ref):
    w_ref[:, : x_ref.shape[0]] = gram_ref[...]
    finish(w_ref, q_ref, occ_ref, out_ref, x_ref)


def per_device(
    ndom, block, conn, bottom, cell_scale, potential, mass, stiffness, interp, occupancy, spectrum
):
    own, node_dev = block.shape
    npc, cells = conn.shape
    gauss = interp.shape[0]
    nodes = up(node_dev, PAD)
    ext = nodes + PAD
    orbs = 2 * own
    rows = up(bottom.shape[0], 8)
    fits = own % (8 * ndom) == 0
    moved = jnp.where(conn >= node_dev, conn + (nodes - node_dev), conn)
    moved = jnp.pad(moved, ((0, LANE - npc), (0, 0)), constant_values=-1).T
    vm = pl.BlockSpec(memory_space=pltpu.VMEM)
    sm = pl.BlockSpec(memory_space=pltpu.SMEM)
    dma = pltpu.SemaphoreType.DMA
    peers = ndom if fits else 1
    share = own // ndom if fits else 8
    density_shape = jax.ShapeDtypeStruct((cells, gauss), F32)
    if fits:
        out_shape = density_shape
    else:
        out_shape = (
            jax.ShapeDtypeStruct((orbs, orbs), F32),
            jax.ShapeDtypeStruct((2, cells, orbs, gauss), BF16),
            jax.ShapeDtypeStruct((2, 8, own), F32),
        )
    buffers = [
        ((ext, ext), BF16),
        ((ext, ext), BF16),
        ((PAD, PAD), F32),
        ((ext, cells * LANE), BF16),
        ((2, ext, cells * LANE), BF16),
        ((LANE, LANE), F32),
        ((gauss, LANE), F32),
        ((own, nodes), F32),
        ((own, nodes), F32),
        ((DEG + 1, PAD, own), F32),
        ((DEG, PAD, own), F32),
        ((DEG + 1, PAD, own), F32),
        ((DEG, PAD, own), F32),
        ((PAD, PAD), F32),
        ((1, nodes), F32),
        ((1, PAD), jnp.int32),
        ((2, own, nodes), F32),
        ((2, PAD, own), F32),
        ((2, 8, own), F32),
        ((2, own, own), F32),
        ((peers, 2, share, own), F32),
        ((2, 2, own, own), F32),
        ((2, orbs, nodes), BF16),
        ((2, cells, orbs, gauss), BF16),
        ((orbs, 2 * orbs), F32),
        ((orbs, orbs), F32),
    ]
    counts = (DEG + 1, DEG + 1, DEG, DEG, 2, 4, 4, peers, peers, peers, peers)
    result = pl.pallas_call(
        functools.partial(filter_kernel, ndom, fits, node_dev, rows),
        name="filter",
        out_shape=out_shape,
        in_specs=[sm] + [vm] * 9,
        out_specs=vm if fits else (vm, vm, vm),
        scratch_shapes=[pltpu.VMEM(*item) for item in buffers] + [dma((n,)) for n in counts],
        compiler_params=pltpu.CompilerParams(
            collective_id=0, has_side_effects=True, vmem_limit_bytes=VLIMIT
        ),
    )(
        spectrum,
        block,
        moved,
        cell_scale[None, :],
        potential,
        stiffness,
        interp,
        bottom[None, :],
        mass[None, :],
        occupancy[None, :],
    )
    if fits:
        return result.T
    gram, quad, occ = result
    gram = lax.psum(gram, "dom") / (ndom * node_dev)
    density = pl.pallas_call(
        density_kernel,
        name="density",
        out_shape=density_shape,
        in_specs=[vm] * 3,
        out_specs=vm,
        scratch_shapes=[pltpu.VMEM((orbs, 2 * orbs), F32), pltpu.VMEM((orbs, orbs), F32)],
        compiler_params=pltpu.CompilerParams(vmem_limit_bytes=VLIMIT),
    )(gram, quad, occ)
    return density.T


def solution(mesh):
    in_specs = (
        P("orb", "dom"),
        P(None, "dom"),
        P("dom"),
        P("dom"),
        P(None, "dom"),
        P("dom"),
        P(),
        P(),
        P("orb"),
        P(),
    )
    out_specs = P(None, "dom")
    return jax.shard_map(
        functools.partial(per_device, mesh.shape["dom"]),
        mesh=mesh,
        in_specs=in_specs,
        out_specs=out_specs,
        check_vma=False,
    )
```

```python
import functools

import jax
import jax.numpy as jnp
from jax import lax
from jax.experimental import pallas as pl
from jax.experimental.pallas import tpu as pltpu
from jax.sharding import PartitionSpec as P

DEG = 3
LANE = 128
PAD = 256
HI = lax.Precision.HIGHEST
MESH = pl.DeviceIdType.MESH
F32 = jnp.float32
BF16 = jnp.bfloat16
NN = (((1,), (0,)), ((), ()))
NT = (((1,), (1,)), ((), ()))
TN = (((0,), (0,)), ((), ()))
TT = (((0,), (1,)), ((), ()))
VLIMIT = 48 * 1024 * 1024


def up(value, unit):
    return -(-value // unit) * unit


def full_dot(left, right, dims=NN):
    return lax.dot_general(left, right, dims, precision=HI, preferred_element_type=F32)


def split2(value):
    high = value.astype(BF16)
    return high, (value - high.astype(F32)).astype(BF16)


def part_dot(left, right, dims=NN):
    return lax.dot_general(left, right, dims, preferred_element_type=F32)


def dot3(left, right, dims=NN):
    high, low = left
    main, rest = right
    return (part_dot(low, main, dims) + part_dot(high, rest, dims)) + part_dot(high, main, dims)


def pick_dot(parts, onehot, dims=NN):
    high, low = parts
    return part_dot(low, onehot, dims) + part_dot(high, onehot, dims)


def cell_terms(conn_ref, scale_ref, pot_ref, stiff_ref, interp_ref, gt_ref, w_ref, k_ref, b_ref):
    ext = gt_ref.shape[0]
    cells = conn_ref.shape[0]
    npc = stiff_ref.shape[0]
    k_ref[...] = jnp.zeros_like(k_ref)
    k_ref[:npc, :npc] = stiff_ref[...]
    b_ref[...] = jnp.zeros_like(b_ref)
    b_ref[:, :npc] = interp_ref[...]
    interp = b_ref[...]
    parts = split2(interp)
    rows = lax.broadcasted_iota(jnp.int32, (ext, LANE), 0)
    for cell in range(cells):
        cols = slice(cell * LANE, (cell + 1) * LANE)
        hot = (rows == conn_ref[cell : cell + 1, :]).astype(F32).astype(BF16)
        gt_ref[:, cols] = hot
        local = dot3(parts, split2(interp * pot_ref[:, cell : cell + 1]), TN)
        local = local + k_ref[...] * scale_ref[0:1, cell : cell + 1]
        both = part_dot(hot, jnp.concatenate(split2(local), axis=1)).astype(BF16)
        w_ref[0, :, cols] = both[:, :LANE]
        w_ref[1, :, cols] = both[:, LANE:]


def assemble(first, second, ah_ref, al_ref, gt_ref, w_ref):
    here, there = slice(first, first + PAD), slice(second, second + PAD)
    hot = gt_ref[there, :]
    block = part_dot(w_ref[1, here, :], hot, NT) + part_dot(w_ref[0, here, :], hot, NT)
    ah_ref[here, there], al_ref[here, there] = split2(block)
    if second > first:
        ah_ref[there, here], al_ref[there, here] = split2(block.T)
    return block


def filter_kernel(ndom, fits, node_dev, rows, *refs):
    spec_ref, v_ref, conn_ref, scale_ref, pot_ref, stiff_ref, interp_ref = refs[:7]
    bottom_ref, mass_ref, occ_ref = refs[7:10]
    outs = 1 if fits else 3
    outputs = refs[10 : 10 + outs]
    scratch = refs[10 + outs :]
    ah_ref, al_ref, edge_block, gt_ref, w_ref, k_ref, b_ref = scratch[:7]
    cur, prev, vb, rb, gslot, rslot, kp, mass_row, bottom_row = scratch[7:16]
    vall, ghosts, occs, gp, rs, gall, vp, qp, work, inverse_ref, vin, near = scratch[16:28]
    (fsend, frecv, rsend, rrecv, ksem, psend, precv, ssend, srecv, gsend, grecv, insem) = (
        scratch[28:]
    )
    d = lax.axis_index("dom")
    o = lax.axis_index("orb")
    other = 1 - o
    own = v_ref.shape[0]
    nodes = cur.shape[1]
    cells = conn_ref.shape[0]
    has_prev = d > 0
    has_next = d < ndom - 1
    before = lax.rem(d + ndom - 1, ndom)
    after = lax.rem(d + 1, ndom)

    fetch = pltpu.make_async_copy(v_ref, vin, insem.at[0])
    fetch.start()
    gslot[...] = jnp.zeros_like(gslot)
    rslot[...] = jnp.zeros_like(rslot)
    kp[...] = jnp.zeros_like(kp)
    ghosts[...] = jnp.zeros_like(ghosts)

    barrier = pltpu.get_barrier_semaphore()
    pl.semaphore_signal(
        barrier, inc=1, device_id={"dom": d, "orb": other}, device_id_type=MESH
    )
    if fits:

        def greet(k, carry):
            pl.semaphore_signal(
                barrier,
                inc=1,
                device_id={"dom": lax.rem(d + k, ndom), "orb": o},
                device_id_type=MESH,
            )
            return carry

        lax.fori_loop(1, ndom, greet, 0)
    else:
        for ok, peer in ((has_prev, before), (has_next, after)):

            @pl.when(ok)
            def _():
                pl.semaphore_signal(
                    barrier, inc=1, device_id={"dom": peer, "orb": o}, device_id_type=MESH
                )

    cell_terms(
        conn_ref, scale_ref, pot_ref, stiff_ref, interp_ref, gt_ref, w_ref, k_ref, b_ref
    )
    edge_block[...] = assemble(nodes, nodes, ah_ref, al_ref, gt_ref, w_ref)
    halfwidth = (spec_ref[1] - spec_ref[0]) / 2.0
    centre = (spec_ref[1] + spec_ref[0]) / 2.0
    cur[...] = jnp.zeros_like(cur)
    fetch.wait()
    cur[:, :node_dev] = vin[...]
    mass_row[...] = jnp.ones_like(mass_row)
    mass_row[:, :node_dev] = mass_ref[...]
    bottom_row[...] = jnp.full_like(bottom_row, -1)
    bottom_row[:, : bottom_ref.shape[1]] = bottom_ref[...]
    occs[o] = jnp.broadcast_to(occ_ref[...], occs.shape[1:])
    mass = mass_row[...]
    over_mass = 1.0 / (mass * halfwidth)
    shift = centre / halfwidth
    hot = (
        lax.broadcasted_iota(jnp.int32, (nodes, PAD), 0) == bottom_row[...]
    ).astype(F32).astype(BF16)

    if fits:
        pl.semaphore_wait(barrier, ndom)
    else:
        for ok in (has_prev, has_next):

            @pl.when(ok)
            def _():
                pl.semaphore_wait(barrier, 1)

        pl.semaphore_wait(barrier, 1)

    def remote(src, dst, send, recv, dom, orb):
        return pltpu.make_async_remote_copy(
            src_ref=src,
            dst_ref=dst,
            send_sem=send,
            recv_sem=recv,
            device_id={"dom": dom, "orb": orb},
            device_id_type=MESH,
        )

    some = pl.ds(0, rows)

    def face(step):
        return remote(
            vb.at[step, some], gslot.at[step, some], fsend.at[step], frecv.at[step], before, o
        )

    def rim(step):
        return remote(
            rb.at[step, some], rslot.at[step, some], rsend.at[step], rrecv.at[step], after, o
        )

    corner = remote(edge_block.at[some], kp.at[some], ksem.at[0], ksem.at[1], after, o)

    def send_face(step, parts):
        vb[step] = part_dot(hot, parts[1], TT) + part_dot(hot, parts[0], TT)

        @pl.when(has_prev)
        def _():
            face(step).start()

    def send_rim(step, parts):
        rb[step] = dot3((ah_ref[nodes:, :nodes], al_ref[nodes:, :nodes]), parts, NT)

        @pl.when(has_next)
        def _():
            rim(step).start()

    @pl.when(has_next)
    def _():
        corner.start()

    parts = split2(cur[...])
    send_face(0, parts)
    occ_copy = remote(occs.at[o], occs.at[o], psend.at[0], precv.at[0], d, other)
    occ_copy.start()
    for first in range(0, nodes, PAD):
        assemble(first, nodes, ah_ref, al_ref, gt_ref, w_ref)
    send_rim(0, parts)
    for first in range(0, nodes, PAD):
        for second in range(first, nodes, PAD):
            assemble(first, second, ah_ref, al_ref, gt_ref, w_ref)

    for step in range(DEG):
        value = cur[...]
        parts = split2(value)
        if step > 0:
            send_face(step, parts)
            send_rim(step, parts)
        total = dot3(parts, (ah_ref[:nodes, :nodes], al_ref[:nodes, :nodes]))
        if step == 0:

            @pl.when(has_prev)
            def _():
                corner.wait_recv()

        extra = dot3(split2(kp[...]), split2(vb[step]))

        @pl.when(has_next)
        def _():
            face(step).wait_recv()

        total = total + dot3(
            split2(gslot[step]), (ah_ref[nodes:, :nodes], al_ref[nodes:, :nodes]), TN
        )

        @pl.when(has_prev)
        def _():
            rim(step).wait_recv()

        total = total + pick_dot(split2(extra + rslot[step]), hot, TT)
        applied = total * over_mass - shift * value
        if step > 0:
            applied = 2.0 * applied - prev[...]
        prev[...] = value
        cur[...] = applied

    value = cur[...]
    vall[o] = value
    half = remote(vall.at[o], vall.at[o], psend.at[1], precv.at[1], d, other)
    half.start()
    parts = split2(value)
    send_face(DEG, parts)
    weighted = split2(value * mass)
    gp[o] = dot3(weighted, parts, NT)
    half.wait_recv()
    gp[other] = dot3(weighted, split2(vall[other]), NT)

    def run(action):
        lax.fori_loop(1, ndom, lambda k, carry: (action(k), carry)[1], 0)

    if fits:
        share = own // ndom
        mine = pl.ds(pl.multiple_of(d * share, 8), share)

        def scatter(k):
            peer = lax.rem(d + k, ndom)
            return remote(
                gp.at[:, pl.ds(pl.multiple_of(peer * share, 8), share), :],
                rs.at[k],
                ssend.at[k],
                srecv.at[k],
                peer,
                o,
            )

        def gather(k):
            return remote(
                gall.at[o, :, mine, :],
                gall.at[o, :, mine, :],
                gsend.at[k],
                grecv.at[k],
                lax.rem(d + k, ndom),
                o,
            )

        def arrive(k):
            came = lax.rem(d + ndom - k, ndom)
            spot = pl.ds(pl.multiple_of(came * share, 8), share)
            return remote(
                gall.at[o, :, spot, :],
                gall.at[o, :, spot, :],
                gsend.at[k],
                grecv.at[k],
                came,
                o,
            )

        run(lambda k: scatter(k).start())

    for orb in range(2):
        part = slice(orb * own, (orb + 1) * own)
        vp[0, part, :], vp[1, part, :] = split2(vall[orb])
    near[...] = pick_dot((vp[0], vp[1]), gt_ref[:nodes, :])

    @pl.when(has_next)
    def _():
        face(DEG).wait_recv()

    ghosts[o] = gslot[DEG]
    ghost = remote(
        ghosts.at[o, some], ghosts.at[o, some], psend.at[2], precv.at[2], d, other
    )
    ghost.start()
    if fits:
        run(lambda k: scatter(k).wait_recv())
        rs[0] = gp[:, mine, :]
        total = rs[0]
        for k in range(1, ndom):
            total = total + rs[k]
        gall[o, :, mine, :] = total / (ndom * node_dev)
        run(lambda k: gather(k).start())
    ghost.wait_recv()
    far = split2(jnp.concatenate([ghosts[0], ghosts[1]], axis=1))
    basis = split2(b_ref[...])
    for cell in range(cells):
        cols = slice(cell * LANE, (cell + 1) * LANE)
        local = near[:, cols] + pick_dot(far, gt_ref[nodes:, cols], TN)
        qp[0, cell], qp[1, cell] = split2(dot3(split2(local), basis, NT))
    occ_copy.wait_recv()
    if fits:
        run(lambda k: arrive(k).wait_recv())
        swap = remote(gall.at[o], gall.at[o], psend.at[3], precv.at[3], d, other)
        swap.start()
        swap.wait_recv()
        for row in range(2):
            for col in range(2):
                work[row * own : (row + 1) * own, col * own : (col + 1) * own] = gall[row, col]
        finish(work, qp, occs, outputs[0], inverse_ref)
        run(lambda k: scatter(k).wait_send())
        run(lambda k: gather(k).wait_send())
        swap.wait_send()
    else:
        gram_out, q_out, occ_out = outputs
        for row in range(2):
            for col in range(2):
                gram_out[row * own : (row + 1) * own, col * own : (col + 1) * own] = full_dot(
                    vall[row] * mass, vall[col], NT
                )
        q_out[...] = qp[...]
        occ_out[...] = occs[...]

    occ_copy.wait_send()
    half.wait_send()
    ghost.wait_send()
    for step in range(DEG + 1):

        @pl.when(has_prev)
        def _():
            face(step).wait_send()

    for step in range(DEG):

        @pl.when(has_next)
        def _():
            rim(step).wait_send()

    @pl.when(has_next)
    def _():
        corner.wait_send()


def small_inverse(tile, side, size):
    lanes = lax.broadcasted_iota(jnp.int32, tile.shape, 1)
    rows = lax.broadcasted_iota(jnp.int32, tile.shape, 0)
    keep = (lanes >= side * size) & (lanes < (side + 1) * size)
    unit = (lanes - (1 - side) * size == rows).astype(F32)
    work = jnp.where(keep, tile, unit)
    groups = size // 8
    pieces = [work[8 * g : 8 * g + 8] for g in range(groups)]
    below = lax.broadcasted_iota(jnp.int32, (8, LANE), 0)
    panel = 4
    full = (8, LANE)
    for start in range(0, size, panel):
        top, row = divmod(start, 8)
        lane = side * size + start
        head = [pieces[top][row + a : row + a + 1, :] for a in range(panel)]
        line = [jnp.broadcast_to(value, full) for value in head]
        pivot = [
            [
                jnp.broadcast_to(head[a][:, lane + b : lane + b + 1], full) if b >= a else None
                for b in range(panel)
            ]
            for a in range(panel)
        ]
        column = [
            [
                jnp.broadcast_to(pieces[g][:, lane + b : lane + b + 1], full)
                for b in range(panel)
            ]
            for g in range(top, groups)
        ]
        for a in range(panel):
            over = 1.0 / pivot[a][a]
            for g in range(top, groups):
                if g == top and row + a == 7:
                    continue
                terms = column[g - top]
                factor = terms[a] * over
                if g == top:
                    factor = jnp.where(below > row + a, factor, 0.0)
                pieces[g] = pieces[g] - factor * line[a]
                for b in range(a + 1, panel):
                    terms[b] = terms[b] - factor * pivot[a][b]
            for b in range(a + 1, panel):
                factor = pivot[a][b] * over
                line[b] = line[b] - factor * line[a]
                for c in range(b, panel):
                    pivot[b][c] = pivot[b][c] - factor * pivot[a][c]
    work = jnp.concatenate(pieces, axis=0)
    diag = jnp.sum(jnp.where(lanes - side * size == rows, work, 0.0), axis=1, keepdims=True)
    work = work * (1.0 / jnp.sqrt(diag))
    return work[:, (1 - side) * size : (2 - side) * size]


def finish(w_ref, q_ref, occ_ref, out_ref, x_ref):
    orbs = x_ref.shape[0]
    own = occ_ref.shape[2]
    size = 64
    shape = (orbs, orbs)
    eye = lax.broadcasted_iota(jnp.int32, shape, 0) == lax.broadcasted_iota(jnp.int32, shape, 1)
    w_ref[:, orbs:] = eye.astype(F32)
    for first in range(0, orbs, size):
        last = first + size
        base = first // LANE * LANE
        tile = w_ref[first:last, base : base + LANE]
        lower = small_inverse(tile, (first - base) // size, size)
        stop = orbs + up(last, LANE)
        step = full_dot(lower, w_ref[first:last, base:stop])
        x_ref[first:last, :] = jnp.zeros((size, orbs), F32)
        x_ref[first:last, : stop - orbs] = step[:, orbs - base :]
        if last < orbs:
            w_ref[last:, base:stop] = w_ref[last:, base:stop] - full_dot(
                step[:, last - base : orbs - base], step, TN
            )
    inverse = split2(x_ref[...])
    occ = jnp.concatenate([occ_ref[0, 0:1, :own], occ_ref[1, 0:1, :own]], axis=1)
    weight = jnp.sum(jnp.where(eye, occ, 0.0), axis=1, keepdims=True) / orbs
    for cell in range(out_ref.shape[0]):
        ortho = dot3(inverse, (q_ref[0, cell], q_ref[1, cell]))
        out_ref[cell : cell + 1, :] = jnp.sum(weight * (ortho * ortho), axis=0, keepdims=True)


def density_kernel(gram_ref, q_ref, occ_ref, out_ref, w_ref, x_ref):
    w_ref[:, : x_ref.shape[0]] = gram_ref[...]
    finish(w_ref, q_ref, occ_ref, out_ref, x_ref)


def per_device(
    ndom, block, conn, bottom, cell_scale, potential, mass, stiffness, interp, occupancy, spectrum
):
    own, node_dev = block.shape
    npc, cells = conn.shape
    gauss = interp.shape[0]
    nodes = up(node_dev, PAD)
    ext = nodes + PAD
    orbs = 2 * own
    rows = up(bottom.shape[0], 8)
    fits = own % (8 * ndom) == 0
    moved = jnp.where(conn >= node_dev, conn + (nodes - node_dev), conn)
    moved = jnp.pad(moved, ((0, LANE - npc), (0, 0)), constant_values=-1).T
    vm = pl.BlockSpec(memory_space=pltpu.VMEM)
    sm = pl.BlockSpec(memory_space=pltpu.SMEM)
    dma = pltpu.SemaphoreType.DMA
    peers = ndom if fits else 1
    share = own // ndom if fits else 8
    density_shape = jax.ShapeDtypeStruct((cells, gauss), F32)
    if fits:
        out_shape = density_shape
    else:
        out_shape = (
            jax.ShapeDtypeStruct((orbs, orbs), F32),
            jax.ShapeDtypeStruct((2, cells, orbs, gauss), BF16),
            jax.ShapeDtypeStruct((2, 8, own), F32),
        )
    buffers = [
        ((ext, ext), BF16),
        ((ext, ext), BF16),
        ((PAD, PAD), F32),
        ((ext, cells * LANE), BF16),
        ((2, ext, cells * LANE), BF16),
        ((LANE, LANE), F32),
        ((gauss, LANE), F32),
        ((own, nodes), F32),
        ((own, nodes), F32),
        ((DEG + 1, PAD, own), F32),
        ((DEG, PAD, own), F32),
        ((DEG + 1, PAD, own), F32),
        ((DEG, PAD, own), F32),
        ((PAD, PAD), F32),
        ((1, nodes), F32),
        ((1, PAD), jnp.int32),
        ((2, own, nodes), F32),
        ((2, PAD, own), F32),
        ((2, 8, own), F32),
        ((2, own, own), F32),
        ((peers, 2, share, own), F32),
        ((2, 2, own, own), F32),
        ((2, orbs, nodes), BF16),
        ((2, cells, orbs, gauss), BF16),
        ((orbs, 2 * orbs), F32),
        ((orbs, orbs), F32),
        ((own, node_dev), F32),
        ((orbs, cells * LANE), F32),
    ]
    counts = (DEG + 1, DEG + 1, DEG, DEG, 2, 4, 4, peers, peers, peers, peers, 1)
    result = pl.pallas_call(
        functools.partial(filter_kernel, ndom, fits, node_dev, rows),
        name="filter",
        out_shape=out_shape,
        in_specs=[sm, pl.BlockSpec(memory_space=pl.ANY)] + [vm] * 8,
        out_specs=vm if fits else (vm, vm, vm),
        scratch_shapes=[pltpu.VMEM(*item) for item in buffers] + [dma((n,)) for n in counts],
        compiler_params=pltpu.CompilerParams(
            collective_id=0, has_side_effects=True, vmem_limit_bytes=VLIMIT
        ),
    )(
        spectrum,
        block,
        moved,
        cell_scale[None, :],
        potential,
        stiffness,
        interp,
        bottom[None, :],
        mass[None, :],
        occupancy[None, :],
    )
    if fits:
        return result.T
    gram, quad, occ = result
    gram = lax.psum(gram, "dom") / (ndom * node_dev)
    density = pl.pallas_call(
        density_kernel,
        name="density",
        out_shape=density_shape,
        in_specs=[vm] * 3,
        out_specs=vm,
        scratch_shapes=[pltpu.VMEM((orbs, 2 * orbs), F32), pltpu.VMEM((orbs, orbs), F32)],
        compiler_params=pltpu.CompilerParams(vmem_limit_bytes=VLIMIT),
    )(gram, quad, occ)
    return density.T


def solution(mesh):
    in_specs = (
        P("orb", "dom"),
        P(None, "dom"),
        P("dom"),
        P("dom"),
        P(None, "dom"),
        P("dom"),
        P(),
        P(),
        P("orb"),
        P(),
    )
    out_specs = P(None, "dom")
    return jax.shard_map(
        functools.partial(per_device, mesh.shape["dom"]),
        mesh=mesh,
        in_specs=in_specs,
        out_specs=out_specs,
        check_vma=False,
    )
```

```python
import functools

import jax
import jax.numpy as jnp
from jax import lax
from jax.experimental import pallas as pl
from jax.experimental.pallas import tpu as pltpu
from jax.sharding import PartitionSpec as P

DEG = 3
LANE = 128
PAD = 256
HI = lax.Precision.HIGHEST
MESH = pl.DeviceIdType.MESH
F32 = jnp.float32
BF16 = jnp.bfloat16
NN = (((1,), (0,)), ((), ()))
NT = (((1,), (1,)), ((), ()))
TN = (((0,), (0,)), ((), ()))
TT = (((0,), (1,)), ((), ()))
VLIMIT = 48 * 1024 * 1024


def up(value, unit):
    return -(-value // unit) * unit


def full_dot(left, right, dims=NN):
    return lax.dot_general(left, right, dims, precision=HI, preferred_element_type=F32)


def split2(value):
    high = value.astype(BF16)
    return high, (value - high.astype(F32)).astype(BF16)


def part_dot(left, right, dims=NN):
    return lax.dot_general(left, right, dims, preferred_element_type=F32)


def dot3(left, right, dims=NN):
    high, low = left
    main, rest = right
    return (part_dot(low, main, dims) + part_dot(high, rest, dims)) + part_dot(high, main, dims)


def pick_dot(parts, onehot, dims=NN):
    high, low = parts
    return part_dot(low, onehot, dims) + part_dot(high, onehot, dims)


def cell_terms(conn_ref, scale_ref, pot_ref, stiff_ref, interp_ref, gt_ref, w_ref, k_ref, b_ref):
    ext = gt_ref.shape[0]
    cells = conn_ref.shape[0]
    npc = stiff_ref.shape[0]
    k_ref[...] = jnp.zeros_like(k_ref)
    k_ref[:npc, :npc] = stiff_ref[...]
    b_ref[...] = jnp.zeros_like(b_ref)
    b_ref[:, :npc] = interp_ref[...]
    interp = b_ref[...]
    parts = split2(interp)
    rows = lax.broadcasted_iota(jnp.int32, (ext, LANE), 0)
    for cell in range(cells):
        cols = slice(cell * LANE, (cell + 1) * LANE)
        hot = (rows == conn_ref[cell : cell + 1, :]).astype(F32).astype(BF16)
        gt_ref[:, cols] = hot
        local = dot3(parts, split2(interp * pot_ref[:, cell : cell + 1]), TN)
        local = local + k_ref[...] * scale_ref[0:1, cell : cell + 1]
        both = part_dot(hot, jnp.concatenate(split2(local), axis=1)).astype(BF16)
        w_ref[0, :, cols] = both[:, :LANE]
        w_ref[1, :, cols] = both[:, LANE:]


def assemble(first, second, ah_ref, al_ref, gt_ref, w_ref):
    here, there = slice(first, first + PAD), slice(second, second + PAD)
    hot = gt_ref[there, :]
    block = part_dot(w_ref[1, here, :], hot, NT) + part_dot(w_ref[0, here, :], hot, NT)
    ah_ref[here, there], al_ref[here, there] = split2(block)
    if second > first:
        ah_ref[there, here], al_ref[there, here] = split2(block.T)
    return block


def filter_kernel(ndom, fits, node_dev, rows, *refs):
    spec_ref, v_ref, conn_ref, scale_ref, pot_ref, stiff_ref, interp_ref = refs[:7]
    bottom_ref, mass_ref, occ_ref = refs[7:10]
    outs = 1 if fits else 3
    outputs = refs[10 : 10 + outs]
    scratch = refs[10 + outs :]
    ah_ref, al_ref, edge_block, gt_ref, w_ref, k_ref, b_ref = scratch[:7]
    cur, prev, vb, rb, gslot, rslot, kp, mass_row, bottom_row = scratch[7:16]
    vall, ghosts, occs, gp, rs, gall, vp, qp, work, inverse_ref, vin, near = scratch[16:28]
    (fsend, frecv, rsend, rrecv, ksem, psend, precv, ssend, srecv, gsend, grecv, insem, wsend, wrecv) = (
        scratch[28:]
    )
    d = lax.axis_index("dom")
    o = lax.axis_index("orb")
    other = 1 - o
    own = v_ref.shape[0]
    nodes = cur.shape[1]
    cells = conn_ref.shape[0]
    has_prev = d > 0
    has_next = d < ndom - 1
    before = lax.rem(d + ndom - 1, ndom)
    after = lax.rem(d + 1, ndom)

    fetch = pltpu.make_async_copy(v_ref, vin, insem.at[0])
    fetch.start()
    gslot[...] = jnp.zeros_like(gslot)
    rslot[...] = jnp.zeros_like(rslot)
    kp[...] = jnp.zeros_like(kp)
    ghosts[...] = jnp.zeros_like(ghosts)

    barrier = pltpu.get_barrier_semaphore()
    pl.semaphore_signal(
        barrier, inc=1, device_id={"dom": d, "orb": other}, device_id_type=MESH
    )
    if fits:

        def greet(k, carry):
            pl.semaphore_signal(
                barrier,
                inc=1,
                device_id={"dom": lax.rem(d + k, ndom), "orb": o},
                device_id_type=MESH,
            )
            return carry

        lax.fori_loop(1, ndom, greet, 0)
    else:
        for ok, peer in ((has_prev, before), (has_next, after)):

            @pl.when(ok)
            def _():
                pl.semaphore_signal(
                    barrier, inc=1, device_id={"dom": peer, "orb": o}, device_id_type=MESH
                )

    cell_terms(
        conn_ref, scale_ref, pot_ref, stiff_ref, interp_ref, gt_ref, w_ref, k_ref, b_ref
    )
    edge_block[...] = assemble(nodes, nodes, ah_ref, al_ref, gt_ref, w_ref)
    halfwidth = (spec_ref[1] - spec_ref[0]) / 2.0
    centre = (spec_ref[1] + spec_ref[0]) / 2.0
    cur[...] = jnp.zeros_like(cur)
    fetch.wait()
    cur[:, :node_dev] = vin[...]
    mass_row[...] = jnp.ones_like(mass_row)
    mass_row[:, :node_dev] = mass_ref[...]
    bottom_row[...] = jnp.full_like(bottom_row, -1)
    bottom_row[:, : bottom_ref.shape[1]] = bottom_ref[...]
    occs[o] = jnp.broadcast_to(occ_ref[...], occs.shape[1:])
    mass = mass_row[...]
    over_mass = 1.0 / (mass * halfwidth)
    shift = centre / halfwidth
    hot = (
        lax.broadcasted_iota(jnp.int32, (nodes, PAD), 0) == bottom_row[...]
    ).astype(F32).astype(BF16)

    if fits:
        pl.semaphore_wait(barrier, ndom)
    else:
        for ok in (has_prev, has_next):

            @pl.when(ok)
            def _():
                pl.semaphore_wait(barrier, 1)

        pl.semaphore_wait(barrier, 1)

    def remote(src, dst, send, recv, dom, orb):
        return pltpu.make_async_remote_copy(
            src_ref=src,
            dst_ref=dst,
            send_sem=send,
            recv_sem=recv,
            device_id={"dom": dom, "orb": orb},
            device_id_type=MESH,
        )

    some = pl.ds(0, rows)

    def face(step):
        return remote(
            vb.at[step, some], gslot.at[step, some], fsend.at[step], frecv.at[step], before, o
        )

    def rim(step):
        return remote(
            rb.at[step, some], rslot.at[step, some], rsend.at[step], rrecv.at[step], after, o
        )

    corner = remote(edge_block.at[some], kp.at[some], ksem.at[0], ksem.at[1], after, o)

    def send_face(step, parts):
        vb[step] = part_dot(hot, parts[1], TT) + part_dot(hot, parts[0], TT)

        @pl.when(has_prev)
        def _():
            face(step).start()

    def send_rim(step, parts):
        rb[step] = dot3((ah_ref[nodes:, :nodes], al_ref[nodes:, :nodes]), parts, NT)

        @pl.when(has_next)
        def _():
            rim(step).start()

    @pl.when(has_next)
    def _():
        corner.start()

    parts = split2(cur[...])
    send_face(0, parts)
    occ_copy = remote(occs.at[o], occs.at[o], psend.at[0], precv.at[0], d, other)
    occ_copy.start()
    for first in range(0, nodes, PAD):
        assemble(first, nodes, ah_ref, al_ref, gt_ref, w_ref)
    send_rim(0, parts)
    for first in range(0, nodes, PAD):
        for second in range(first, nodes, PAD):
            assemble(first, second, ah_ref, al_ref, gt_ref, w_ref)

    for step in range(DEG):
        value = cur[...]
        parts = split2(value)
        if step > 0:
            send_face(step, parts)
            send_rim(step, parts)
        total = dot3(parts, (ah_ref[:nodes, :nodes], al_ref[:nodes, :nodes]))
        if step == 0:

            @pl.when(has_prev)
            def _():
                corner.wait_recv()

        extra = dot3(split2(kp[...]), split2(vb[step]))

        @pl.when(has_next)
        def _():
            face(step).wait_recv()

        total = total + dot3(
            split2(gslot[step]), (ah_ref[nodes:, :nodes], al_ref[nodes:, :nodes]), TN
        )

        @pl.when(has_prev)
        def _():
            rim(step).wait_recv()

        total = total + pick_dot(split2(extra + rslot[step]), hot, TT)
        applied = total * over_mass - shift * value
        if step > 0:
            applied = 2.0 * applied - prev[...]
        prev[...] = value
        cur[...] = applied

    value = cur[...]
    vall[o] = value
    half = remote(vall.at[o], vall.at[o], psend.at[1], precv.at[1], d, other)
    half.start()
    parts = split2(value)
    send_face(DEG, parts)
    weighted = split2(value * mass)
    gp[o] = dot3(weighted, parts, NT)
    half.wait_recv()
    gp[other] = dot3(weighted, split2(vall[other]), NT)

    def run(action):
        lax.fori_loop(1, ndom, lambda k, carry: (action(k), carry)[1], 0)

    if fits:
        share = own // ndom
        mine = pl.ds(pl.multiple_of(d * share, 8), share)

        def scatter(k):
            peer = lax.rem(d + k, ndom)
            return remote(
                gp.at[:, pl.ds(pl.multiple_of(peer * share, 8), share), :],
                rs.at[k],
                ssend.at[k],
                srecv.at[k],
                peer,
                o,
            )

        def gather(k):
            return remote(
                gall.at[o, :, mine, :],
                gall.at[o, :, mine, :],
                gsend.at[k],
                grecv.at[k],
                lax.rem(d + k, ndom),
                o,
            )

        def arrive(k):
            came = lax.rem(d + ndom - k, ndom)
            spot = pl.ds(pl.multiple_of(came * share, 8), share)
            return remote(
                gall.at[o, :, spot, :],
                gall.at[o, :, spot, :],
                gsend.at[k],
                grecv.at[k],
                came,
                o,
            )

        def forward(k):
            spot = pl.ds(pl.multiple_of(lax.rem(d + ndom - k, ndom) * share, 8), share)
            return remote(
                gall.at[o, :, spot, :],
                gall.at[o, :, spot, :],
                wsend.at[k],
                wrecv.at[k],
                d,
                other,
            )

        run(lambda k: scatter(k).start())

    for orb in range(2):
        part = slice(orb * own, (orb + 1) * own)
        vp[0, part, :], vp[1, part, :] = split2(vall[orb])
    near[...] = pick_dot((vp[0], vp[1]), gt_ref[:nodes, :])

    @pl.when(has_next)
    def _():
        face(DEG).wait_recv()

    ghosts[o] = gslot[DEG]
    ghost = remote(
        ghosts.at[o, some], ghosts.at[o, some], psend.at[2], precv.at[2], d, other
    )
    ghost.start()
    if fits:
        run(lambda k: scatter(k).wait_recv())
        rs[0] = gp[:, mine, :]
        total = rs[0]
        for k in range(1, ndom):
            total = total + rs[k]
        gall[o, :, mine, :] = total / (ndom * node_dev)
        run(lambda k: gather(k).start())
        forward(0).start()
    ghost.wait_recv()
    far = split2(jnp.concatenate([ghosts[0], ghosts[1]], axis=1))
    basis = split2(b_ref[...])
    for cell in range(cells):
        cols = slice(cell * LANE, (cell + 1) * LANE)
        local = near[:, cols] + pick_dot(far, gt_ref[nodes:, cols], TN)
        qp[0, cell], qp[1, cell] = split2(dot3(split2(local), basis, NT))
    occ_copy.wait_recv()
    if fits:

        def pass_on(k):
            arrive(k).wait_recv()
            forward(k).start()

        run(pass_on)
        run(lambda k: forward(k).wait_recv())
        forward(0).wait_recv()
        for row in range(2):
            for col in range(2):
                work[row * own : (row + 1) * own, col * own : (col + 1) * own] = gall[row, col]
        finish(work, qp, occs, outputs[0], inverse_ref)
        run(lambda k: scatter(k).wait_send())
        run(lambda k: gather(k).wait_send())
        run(lambda k: forward(k).wait_send())
        forward(0).wait_send()
    else:
        gram_out, q_out, occ_out = outputs
        for row in range(2):
            for col in range(2):
                gram_out[row * own : (row + 1) * own, col * own : (col + 1) * own] = full_dot(
                    vall[row] * mass, vall[col], NT
                )
        q_out[...] = qp[...]
        occ_out[...] = occs[...]

    occ_copy.wait_send()
    half.wait_send()
    ghost.wait_send()
    for step in range(DEG + 1):

        @pl.when(has_prev)
        def _():
            face(step).wait_send()

    for step in range(DEG):

        @pl.when(has_next)
        def _():
            rim(step).wait_send()

    @pl.when(has_next)
    def _():
        corner.wait_send()


def small_inverse(tile, side, size):
    lanes = lax.broadcasted_iota(jnp.int32, tile.shape, 1)
    rows = lax.broadcasted_iota(jnp.int32, tile.shape, 0)
    keep = (lanes >= side * size) & (lanes < (side + 1) * size)
    unit = (lanes - (1 - side) * size == rows).astype(F32)
    work = jnp.where(keep, tile, unit)
    groups = size // 8
    pieces = [work[8 * g : 8 * g + 8] for g in range(groups)]
    below = lax.broadcasted_iota(jnp.int32, (8, LANE), 0)
    panel = 4
    full = (8, LANE)
    for start in range(0, size, panel):
        top, row = divmod(start, 8)
        lane = side * size + start
        head = [pieces[top][row + a : row + a + 1, :] for a in range(panel)]
        line = [jnp.broadcast_to(value, full) for value in head]
        pivot = [
            [
                jnp.broadcast_to(head[a][:, lane + b : lane + b + 1], full) if b >= a else None
                for b in range(panel)
            ]
            for a in range(panel)
        ]
        column = [
            [
                jnp.broadcast_to(pieces[g][:, lane + b : lane + b + 1], full)
                for b in range(panel)
            ]
            for g in range(top, groups)
        ]
        for a in range(panel):
            over = 1.0 / pivot[a][a]
            for g in range(top, groups):
                if g == top and row + a == 7:
                    continue
                terms = column[g - top]
                factor = terms[a] * over
                if g == top:
                    factor = jnp.where(below > row + a, factor, 0.0)
                pieces[g] = pieces[g] - factor * line[a]
                for b in range(a + 1, panel):
                    terms[b] = terms[b] - factor * pivot[a][b]
            for b in range(a + 1, panel):
                factor = pivot[a][b] * over
                line[b] = line[b] - factor * line[a]
                for c in range(b, panel):
                    pivot[b][c] = pivot[b][c] - factor * pivot[a][c]
    work = jnp.concatenate(pieces, axis=0)
    diag = jnp.sum(jnp.where(lanes - side * size == rows, work, 0.0), axis=1, keepdims=True)
    work = work * (1.0 / jnp.sqrt(diag))
    return work[:, (1 - side) * size : (2 - side) * size]


def finish(w_ref, q_ref, occ_ref, out_ref, x_ref):
    orbs = x_ref.shape[0]
    own = occ_ref.shape[2]
    size = 64
    shape = (orbs, orbs)
    eye = lax.broadcasted_iota(jnp.int32, shape, 0) == lax.broadcasted_iota(jnp.int32, shape, 1)
    w_ref[:, orbs:] = eye.astype(F32)
    for first in range(0, orbs, size):
        last = first + size
        base = first // LANE * LANE
        tile = w_ref[first:last, base : base + LANE]
        lower = small_inverse(tile, (first - base) // size, size)
        stop = orbs + up(last, LANE)
        step = full_dot(lower, w_ref[first:last, base:stop])
        x_ref[first:last, :] = jnp.zeros((size, orbs), F32)
        x_ref[first:last, : stop - orbs] = step[:, orbs - base :]
        if last < orbs:
            w_ref[last:, base:stop] = w_ref[last:, base:stop] - full_dot(
                step[:, last - base : orbs - base], step, TN
            )
    inverse = split2(x_ref[...])
    occ = jnp.concatenate([occ_ref[0, 0:1, :own], occ_ref[1, 0:1, :own]], axis=1)
    weight = jnp.sum(jnp.where(eye, occ, 0.0), axis=1, keepdims=True) / orbs
    for cell in range(out_ref.shape[0]):
        ortho = dot3(inverse, (q_ref[0, cell], q_ref[1, cell]))
        out_ref[cell : cell + 1, :] = jnp.sum(weight * (ortho * ortho), axis=0, keepdims=True)


def density_kernel(gram_ref, q_ref, occ_ref, out_ref, w_ref, x_ref):
    w_ref[:, : x_ref.shape[0]] = gram_ref[...]
    finish(w_ref, q_ref, occ_ref, out_ref, x_ref)


def per_device(
    ndom, block, conn, bottom, cell_scale, potential, mass, stiffness, interp, occupancy, spectrum
):
    own, node_dev = block.shape
    npc, cells = conn.shape
    gauss = interp.shape[0]
    nodes = up(node_dev, PAD)
    ext = nodes + PAD
    orbs = 2 * own
    rows = up(bottom.shape[0], 8)
    fits = own % (8 * ndom) == 0
    moved = jnp.where(conn >= node_dev, conn + (nodes - node_dev), conn)
    moved = jnp.pad(moved, ((0, LANE - npc), (0, 0)), constant_values=-1).T
    vm = pl.BlockSpec(memory_space=pltpu.VMEM)
    sm = pl.BlockSpec(memory_space=pltpu.SMEM)
    dma = pltpu.SemaphoreType.DMA
    peers = ndom if fits else 1
    share = own // ndom if fits else 8
    density_shape = jax.ShapeDtypeStruct((cells, gauss), F32)
    if fits:
        out_shape = density_shape
    else:
        out_shape = (
            jax.ShapeDtypeStruct((orbs, orbs), F32),
            jax.ShapeDtypeStruct((2, cells, orbs, gauss), BF16),
            jax.ShapeDtypeStruct((2, 8, own), F32),
        )
    buffers = [
        ((ext, ext), BF16),
        ((ext, ext), BF16),
        ((PAD, PAD), F32),
        ((ext, cells * LANE), BF16),
        ((2, ext, cells * LANE), BF16),
        ((LANE, LANE), F32),
        ((gauss, LANE), F32),
        ((own, nodes), F32),
        ((own, nodes), F32),
        ((DEG + 1, PAD, own), F32),
        ((DEG, PAD, own), F32),
        ((DEG + 1, PAD, own), F32),
        ((DEG, PAD, own), F32),
        ((PAD, PAD), F32),
        ((1, nodes), F32),
        ((1, PAD), jnp.int32),
        ((2, own, nodes), F32),
        ((2, PAD, own), F32),
        ((2, 8, own), F32),
        ((2, own, own), F32),
        ((peers, 2, share, own), F32),
        ((2, 2, own, own), F32),
        ((2, orbs, nodes), BF16),
        ((2, cells, orbs, gauss), BF16),
        ((orbs, 2 * orbs), F32),
        ((orbs, orbs), F32),
        ((own, node_dev), F32),
        ((orbs, cells * LANE), F32),
    ]
    counts = (DEG + 1, DEG + 1, DEG, DEG, 2, 4, 4, peers, peers, peers, peers, 1, peers, peers)
    result = pl.pallas_call(
        functools.partial(filter_kernel, ndom, fits, node_dev, rows),
        name="filter",
        out_shape=out_shape,
        in_specs=[sm, pl.BlockSpec(memory_space=pl.ANY)] + [vm] * 8,
        out_specs=vm if fits else (vm, vm, vm),
        scratch_shapes=[pltpu.VMEM(*item) for item in buffers] + [dma((n,)) for n in counts],
        compiler_params=pltpu.CompilerParams(
            collective_id=0, has_side_effects=True, vmem_limit_bytes=VLIMIT
        ),
    )(
        spectrum,
        block,
        moved,
        cell_scale[None, :],
        potential,
        stiffness,
        interp,
        bottom[None, :],
        mass[None, :],
        occupancy[None, :],
    )
    if fits:
        return result.T
    gram, quad, occ = result
    gram = lax.psum(gram, "dom") / (ndom * node_dev)
    density = pl.pallas_call(
        density_kernel,
        name="density",
        out_shape=density_shape,
        in_specs=[vm] * 3,
        out_specs=vm,
        scratch_shapes=[pltpu.VMEM((orbs, 2 * orbs), F32), pltpu.VMEM((orbs, orbs), F32)],
        compiler_params=pltpu.CompilerParams(vmem_limit_bytes=VLIMIT),
    )(gram, quad, occ)
    return density.T


def solution(mesh):
    in_specs = (
        P("orb", "dom"),
        P(None, "dom"),
        P("dom"),
        P("dom"),
        P(None, "dom"),
        P("dom"),
        P(),
        P(),
        P("orb"),
        P(),
    )
    out_specs = P(None, "dom")
    return jax.shard_map(
        functools.partial(per_device, mesh.shape["dom"]),
        mesh=mesh,
        in_specs=in_specs,
        out_specs=out_specs,
        check_vma=False,
    )
```

```python
import functools

import jax
import jax.numpy as jnp
from jax import lax
from jax.experimental import pallas as pl
from jax.experimental.pallas import tpu as pltpu
from jax.sharding import PartitionSpec as P

DEG = 3
LANE = 128
PAD = 256
HI = lax.Precision.HIGHEST
MESH = pl.DeviceIdType.MESH
F32 = jnp.float32
BF16 = jnp.bfloat16
NN = (((1,), (0,)), ((), ()))
NT = (((1,), (1,)), ((), ()))
TN = (((0,), (0,)), ((), ()))
TT = (((0,), (1,)), ((), ()))
VLIMIT = 48 * 1024 * 1024


def up(value, unit):
    return -(-value // unit) * unit


def full_dot(left, right, dims=NN):
    return lax.dot_general(left, right, dims, precision=HI, preferred_element_type=F32)


def split2(value):
    high = value.astype(BF16)
    return high, (value - high.astype(F32)).astype(BF16)


def part_dot(left, right, dims=NN):
    return lax.dot_general(left, right, dims, preferred_element_type=F32)


def dot3(left, right, dims=NN):
    high, low = left
    main, rest = right
    return (part_dot(low, main, dims) + part_dot(high, rest, dims)) + part_dot(high, main, dims)


def pick_dot(parts, onehot, dims=NN):
    high, low = parts
    return part_dot(low, onehot, dims) + part_dot(high, onehot, dims)


def cell_terms(conn_ref, scale_ref, pot_ref, stiff_ref, interp_ref, gt_ref, w_ref, k_ref, b_ref):
    ext = gt_ref.shape[0]
    cells = conn_ref.shape[0]
    npc = stiff_ref.shape[0]
    k_ref[...] = jnp.zeros_like(k_ref)
    k_ref[:npc, :npc] = stiff_ref[...]
    b_ref[...] = jnp.zeros_like(b_ref)
    b_ref[:, :npc] = interp_ref[...]
    interp = b_ref[...]
    parts = split2(interp)
    rows = lax.broadcasted_iota(jnp.int32, (ext, LANE), 0)
    for cell in range(cells):
        cols = slice(cell * LANE, (cell + 1) * LANE)
        hot = (rows == conn_ref[cell : cell + 1, :]).astype(F32).astype(BF16)
        gt_ref[:, cols] = hot
        local = dot3(parts, split2(interp * pot_ref[:, cell : cell + 1]), TN)
        local = local + k_ref[...] * scale_ref[0:1, cell : cell + 1]
        both = part_dot(hot, jnp.concatenate(split2(local), axis=1)).astype(BF16)
        w_ref[0, :, cols] = both[:, :LANE]
        w_ref[1, :, cols] = both[:, LANE:]


def assemble(first, second, ah_ref, al_ref, gt_ref, w_ref):
    here, there = slice(first, first + PAD), slice(second, second + PAD)
    hot = gt_ref[there, :]
    block = part_dot(w_ref[1, here, :], hot, NT) + part_dot(w_ref[0, here, :], hot, NT)
    ah_ref[here, there], al_ref[here, there] = split2(block)
    if second > first:
        ah_ref[there, here], al_ref[there, here] = split2(block.T)
    return block


def filter_kernel(ndom, fits, node_dev, rows, *refs):
    spec_ref, v_ref, conn_ref, scale_ref, pot_ref, stiff_ref, interp_ref = refs[:7]
    bottom_ref, mass_ref, occ_ref = refs[7:10]
    outs = 1 if fits else 3
    outputs = refs[10 : 10 + outs]
    scratch = refs[10 + outs :]
    ah_ref, al_ref, edge_block, gt_ref, w_ref, k_ref, b_ref = scratch[:7]
    cur, prev, vb, rb, gslot, rslot, kp, mass_row, bottom_row = scratch[7:16]
    vall, ghosts, occs, gp, rs, gall, vp, qp, work, inverse_ref, vin, near = scratch[16:28]
    (fsend, frecv, rsend, rrecv, ksem, psend, precv, ssend, srecv, gsend, grecv, insem) = (
        scratch[28:]
    )
    d = lax.axis_index("dom")
    o = lax.axis_index("orb")
    other = 1 - o
    own = v_ref.shape[0]
    nodes = cur.shape[1]
    cells = conn_ref.shape[0]
    has_prev = d > 0
    has_next = d < ndom - 1
    before = lax.rem(d + ndom - 1, ndom)
    after = lax.rem(d + 1, ndom)

    fetch = pltpu.make_async_copy(v_ref, vin, insem.at[0])
    fetch.start()
    gslot[...] = jnp.zeros_like(gslot)
    rslot[...] = jnp.zeros_like(rslot)
    kp[...] = jnp.zeros_like(kp)
    ghosts[...] = jnp.zeros_like(ghosts)

    barrier = pltpu.get_barrier_semaphore()
    pl.semaphore_signal(
        barrier, inc=1, device_id={"dom": d, "orb": other}, device_id_type=MESH
    )
    if fits:

        def greet(k, carry):
            pl.semaphore_signal(
                barrier,
                inc=1,
                device_id={"dom": lax.rem(d + k, ndom), "orb": o},
                device_id_type=MESH,
            )
            return carry

        lax.fori_loop(1, ndom, greet, 0)
    else:
        for ok, peer in ((has_prev, before), (has_next, after)):

            @pl.when(ok)
            def _():
                pl.semaphore_signal(
                    barrier, inc=1, device_id={"dom": peer, "orb": o}, device_id_type=MESH
                )

    cell_terms(
        conn_ref, scale_ref, pot_ref, stiff_ref, interp_ref, gt_ref, w_ref, k_ref, b_ref
    )
    edge_block[...] = assemble(nodes, nodes, ah_ref, al_ref, gt_ref, w_ref)
    halfwidth = (spec_ref[1] - spec_ref[0]) / 2.0
    centre = (spec_ref[1] + spec_ref[0]) / 2.0
    cur[...] = jnp.zeros_like(cur)
    fetch.wait()
    cur[:, :node_dev] = vin[...]
    mass_row[...] = jnp.ones_like(mass_row)
    mass_row[:, :node_dev] = mass_ref[...]
    bottom_row[...] = jnp.full_like(bottom_row, -1)
    bottom_row[:, : bottom_ref.shape[1]] = bottom_ref[...]
    occs[o] = jnp.broadcast_to(occ_ref[...], occs.shape[1:])
    mass = mass_row[...]
    over_mass = 1.0 / (mass * halfwidth)
    shift = centre / halfwidth
    hot = (
        lax.broadcasted_iota(jnp.int32, (nodes, PAD), 0) == bottom_row[...]
    ).astype(F32).astype(BF16)

    if fits:
        pl.semaphore_wait(barrier, ndom)
    else:
        for ok in (has_prev, has_next):

            @pl.when(ok)
            def _():
                pl.semaphore_wait(barrier, 1)

        pl.semaphore_wait(barrier, 1)

    def remote(src, dst, send, recv, dom, orb):
        return pltpu.make_async_remote_copy(
            src_ref=src,
            dst_ref=dst,
            send_sem=send,
            recv_sem=recv,
            device_id={"dom": dom, "orb": orb},
            device_id_type=MESH,
        )

    some = pl.ds(0, rows)

    def face(step):
        return remote(
            vb.at[step, some], gslot.at[step, some], fsend.at[step], frecv.at[step], before, o
        )

    def rim(step):
        return remote(
            rb.at[step, some], rslot.at[step, some], rsend.at[step], rrecv.at[step], after, o
        )

    corner = remote(edge_block.at[some], kp.at[some], ksem.at[0], ksem.at[1], after, o)

    def send_face(step, parts):
        vb[step] = part_dot(hot, parts[1], TT) + part_dot(hot, parts[0], TT)

        @pl.when(has_prev)
        def _():
            face(step).start()

    def send_rim(step, parts):
        rb[step] = dot3((ah_ref[nodes:, :nodes], al_ref[nodes:, :nodes]), parts, NT)

        @pl.when(has_next)
        def _():
            rim(step).start()

    @pl.when(has_next)
    def _():
        corner.start()

    parts = split2(cur[...])
    send_face(0, parts)
    occ_copy = remote(occs.at[o], occs.at[o], psend.at[0], precv.at[0], d, other)
    occ_copy.start()
    for first in range(0, nodes, PAD):
        assemble(first, nodes, ah_ref, al_ref, gt_ref, w_ref)
    send_rim(0, parts)
    for first in range(0, nodes, PAD):
        for second in range(first, nodes, PAD):
            assemble(first, second, ah_ref, al_ref, gt_ref, w_ref)

    for step in range(DEG):
        value = cur[...]
        parts = split2(value)
        if step > 0:
            send_face(step, parts)
            send_rim(step, parts)
        total = dot3(parts, (ah_ref[:nodes, :nodes], al_ref[:nodes, :nodes]))
        if step == 0:

            @pl.when(has_prev)
            def _():
                corner.wait_recv()

        extra = dot3(split2(kp[...]), split2(vb[step]))

        @pl.when(has_next)
        def _():
            face(step).wait_recv()

        total = total + dot3(
            split2(gslot[step]), (ah_ref[nodes:, :nodes], al_ref[nodes:, :nodes]), TN
        )

        @pl.when(has_prev)
        def _():
            rim(step).wait_recv()

        total = total + pick_dot(split2(extra + rslot[step]), hot, TT)
        applied = total * over_mass - shift * value
        if step > 0:
            applied = 2.0 * applied - prev[...]
        prev[...] = value
        cur[...] = applied

    value = cur[...]
    vall[o] = value
    half = remote(vall.at[o], vall.at[o], psend.at[1], precv.at[1], d, other)
    half.start()
    parts = split2(value)
    send_face(DEG, parts)
    weighted = split2(value * mass)
    gp[o] = dot3(weighted, parts, NT)
    half.wait_recv()
    gp[other] = dot3(weighted, split2(vall[other]), NT)

    def run(action):
        lax.fori_loop(1, ndom, lambda k, carry: (action(k), carry)[1], 0)

    if fits:
        share = own // ndom
        mine = pl.ds(pl.multiple_of(d * share, 8), share)

        def scatter(k):
            peer = lax.rem(d + k, ndom)
            return remote(
                gp.at[:, pl.ds(pl.multiple_of(peer * share, 8), share), :],
                rs.at[k],
                ssend.at[k],
                srecv.at[k],
                peer,
                o,
            )

        def gather(k):
            return remote(
                gall.at[o, :, mine, :],
                gall.at[o, :, mine, :],
                gsend.at[k],
                grecv.at[k],
                lax.rem(d + k, ndom),
                o,
            )

        def arrive(k):
            came = lax.rem(d + ndom - k, ndom)
            spot = pl.ds(pl.multiple_of(came * share, 8), share)
            return remote(
                gall.at[o, :, spot, :],
                gall.at[o, :, spot, :],
                gsend.at[k],
                grecv.at[k],
                came,
                o,
            )

        run(lambda k: scatter(k).start())

    for orb in range(2):
        part = slice(orb * own, (orb + 1) * own)
        vp[0, part, :], vp[1, part, :] = split2(vall[orb])
    near[...] = pick_dot((vp[0], vp[1]), gt_ref[:nodes, :])

    @pl.when(has_next)
    def _():
        face(DEG).wait_recv()

    ghosts[o] = gslot[DEG]
    ghost = remote(
        ghosts.at[o, some], ghosts.at[o, some], psend.at[2], precv.at[2], d, other
    )
    ghost.start()
    if fits:
        run(lambda k: scatter(k).wait_recv())
        rs[0] = gp[:, mine, :]
        total = rs[0]
        for k in range(1, ndom):
            total = total + rs[k]
        gall[o, :, mine, :] = total / (ndom * node_dev)
        run(lambda k: gather(k).start())
    ghost.wait_recv()
    far = split2(jnp.concatenate([ghosts[0], ghosts[1]], axis=1))
    basis = split2(b_ref[...])
    for cell in range(cells):
        cols = slice(cell * LANE, (cell + 1) * LANE)
        local = near[:, cols] + pick_dot(far, gt_ref[nodes:, cols], TN)
        qp[0, cell], qp[1, cell] = split2(dot3(split2(local), basis, NT))
    occ_copy.wait_recv()
    if fits:
        run(lambda k: arrive(k).wait_recv())
        swap = remote(gall.at[o], gall.at[o], psend.at[3], precv.at[3], d, other)
        swap.start()
        swap.wait_recv()
        for row in range(2):
            for col in range(2):
                work[row * own : (row + 1) * own, col * own : (col + 1) * own] = gall[row, col]
        finish(work, qp, occs, outputs[0], inverse_ref)
        run(lambda k: scatter(k).wait_send())
        run(lambda k: gather(k).wait_send())
        swap.wait_send()
    else:
        gram_out, q_out, occ_out = outputs
        for row in range(2):
            for col in range(2):
                gram_out[row * own : (row + 1) * own, col * own : (col + 1) * own] = full_dot(
                    vall[row] * mass, vall[col], NT
                )
        q_out[...] = qp[...]
        occ_out[...] = occs[...]

    occ_copy.wait_send()
    half.wait_send()
    ghost.wait_send()
    for step in range(DEG + 1):

        @pl.when(has_prev)
        def _():
            face(step).wait_send()

    for step in range(DEG):

        @pl.when(has_next)
        def _():
            rim(step).wait_send()

    @pl.when(has_next)
    def _():
        corner.wait_send()


def small_inverse(tile, side, size):
    lanes = lax.broadcasted_iota(jnp.int32, tile.shape, 1)
    rows = lax.broadcasted_iota(jnp.int32, tile.shape, 0)
    keep = (lanes >= side * size) & (lanes < (side + 1) * size)
    unit = (lanes - (1 - side) * size == rows).astype(F32)
    work = jnp.where(keep, tile, unit)
    groups = size // 8
    pieces = [work[8 * g : 8 * g + 8] for g in range(groups)]
    below = lax.broadcasted_iota(jnp.int32, (8, LANE), 0)
    panel = 8
    full = (8, LANE)
    for start in range(0, size, panel):
        top, row = divmod(start, 8)
        lane = side * size + start
        head = [pieces[top][row + a : row + a + 1, :] for a in range(panel)]
        line = [jnp.broadcast_to(value, full) for value in head]
        pivot = [
            [
                jnp.broadcast_to(head[a][:, lane + b : lane + b + 1], full) if b >= a else None
                for b in range(panel)
            ]
            for a in range(panel)
        ]
        column = [
            [
                jnp.broadcast_to(pieces[g][:, lane + b : lane + b + 1], full)
                for b in range(panel)
            ]
            for g in range(top, groups)
        ]
        for a in range(panel):
            over = 1.0 / pivot[a][a]
            for g in range(top, groups):
                if g == top and row + a == 7:
                    continue
                terms = column[g - top]
                factor = terms[a] * over
                if g == top:
                    factor = jnp.where(below > row + a, factor, 0.0)
                pieces[g] = pieces[g] - factor * line[a]
                for b in range(a + 1, panel):
                    terms[b] = terms[b] - factor * pivot[a][b]
            for b in range(a + 1, panel):
                factor = pivot[a][b] * over
                line[b] = line[b] - factor * line[a]
                for c in range(b, panel):
                    pivot[b][c] = pivot[b][c] - factor * pivot[a][c]
    work = jnp.concatenate(pieces, axis=0)
    diag = jnp.sum(jnp.where(lanes - side * size == rows, work, 0.0), axis=1, keepdims=True)
    work = work * (1.0 / jnp.sqrt(diag))
    return work[:, (1 - side) * size : (2 - side) * size]


def finish(w_ref, q_ref, occ_ref, out_ref, x_ref):
    orbs = x_ref.shape[0]
    own = occ_ref.shape[2]
    size = 64
    shape = (orbs, orbs)
    eye = lax.broadcasted_iota(jnp.int32, shape, 0) == lax.broadcasted_iota(jnp.int32, shape, 1)
    w_ref[:, orbs:] = eye.astype(F32)
    for first in range(0, orbs, size):
        last = first + size
        base = first // LANE * LANE
        tile = w_ref[first:last, base : base + LANE]
        lower = small_inverse(tile, (first - base) // size, size)
        stop = orbs + up(last, LANE)
        step = full_dot(lower, w_ref[first:last, base:stop])
        x_ref[first:last, :] = jnp.zeros((size, orbs), F32)
        x_ref[first:last, : stop - orbs] = step[:, orbs - base :]
        if last < orbs:
            w_ref[last:, base:stop] = w_ref[last:, base:stop] - full_dot(
                step[:, last - base : orbs - base], step, TN
            )
    inverse = split2(x_ref[...])
    occ = jnp.concatenate([occ_ref[0, 0:1, :own], occ_ref[1, 0:1, :own]], axis=1)
    weight = jnp.sum(jnp.where(eye, occ, 0.0), axis=1, keepdims=True) / orbs
    for cell in range(out_ref.shape[0]):
        ortho = dot3(inverse, (q_ref[0, cell], q_ref[1, cell]))
        out_ref[cell : cell + 1, :] = jnp.sum(weight * (ortho * ortho), axis=0, keepdims=True)


def density_kernel(gram_ref, q_ref, occ_ref, out_ref, w_ref, x_ref):
    w_ref[:, : x_ref.shape[0]] = gram_ref[...]
    finish(w_ref, q_ref, occ_ref, out_ref, x_ref)


def per_device(
    ndom, block, conn, bottom, cell_scale, potential, mass, stiffness, interp, occupancy, spectrum
):
    own, node_dev = block.shape
    npc, cells = conn.shape
    gauss = interp.shape[0]
    nodes = up(node_dev, PAD)
    ext = nodes + PAD
    orbs = 2 * own
    rows = up(bottom.shape[0], 8)
    fits = own % (8 * ndom) == 0
    moved = jnp.where(conn >= node_dev, conn + (nodes - node_dev), conn)
    moved = jnp.pad(moved, ((0, LANE - npc), (0, 0)), constant_values=-1).T
    vm = pl.BlockSpec(memory_space=pltpu.VMEM)
    sm = pl.BlockSpec(memory_space=pltpu.SMEM)
    dma = pltpu.SemaphoreType.DMA
    peers = ndom if fits else 1
    share = own // ndom if fits else 8
    density_shape = jax.ShapeDtypeStruct((cells, gauss), F32)
    if fits:
        out_shape = density_shape
    else:
        out_shape = (
            jax.ShapeDtypeStruct((orbs, orbs), F32),
            jax.ShapeDtypeStruct((2, cells, orbs, gauss), BF16),
            jax.ShapeDtypeStruct((2, 8, own), F32),
        )
    buffers = [
        ((ext, ext), BF16),
        ((ext, ext), BF16),
        ((PAD, PAD), F32),
        ((ext, cells * LANE), BF16),
        ((2, ext, cells * LANE), BF16),
        ((LANE, LANE), F32),
        ((gauss, LANE), F32),
        ((own, nodes), F32),
        ((own, nodes), F32),
        ((DEG + 1, PAD, own), F32),
        ((DEG, PAD, own), F32),
        ((DEG + 1, PAD, own), F32),
        ((DEG, PAD, own), F32),
        ((PAD, PAD), F32),
        ((1, nodes), F32),
        ((1, PAD), jnp.int32),
        ((2, own, nodes), F32),
        ((2, PAD, own), F32),
        ((2, 8, own), F32),
        ((2, own, own), F32),
        ((peers, 2, share, own), F32),
        ((2, 2, own, own), F32),
        ((2, orbs, nodes), BF16),
        ((2, cells, orbs, gauss), BF16),
        ((orbs, 2 * orbs), F32),
        ((orbs, orbs), F32),
        ((own, node_dev), F32),
        ((orbs, cells * LANE), F32),
    ]
    counts = (DEG + 1, DEG + 1, DEG, DEG, 2, 4, 4, peers, peers, peers, peers, 1)
    result = pl.pallas_call(
        functools.partial(filter_kernel, ndom, fits, node_dev, rows),
        name="filter",
        out_shape=out_shape,
        in_specs=[sm, pl.BlockSpec(memory_space=pl.ANY)] + [vm] * 8,
        out_specs=vm if fits else (vm, vm, vm),
        scratch_shapes=[pltpu.VMEM(*item) for item in buffers] + [dma((n,)) for n in counts],
        compiler_params=pltpu.CompilerParams(
            collective_id=0, has_side_effects=True, vmem_limit_bytes=VLIMIT
        ),
    )(
        spectrum,
        block,
        moved,
        cell_scale[None, :],
        potential,
        stiffness,
        interp,
        bottom[None, :],
        mass[None, :],
        occupancy[None, :],
    )
    if fits:
        return result.T
    gram, quad, occ = result
    gram = lax.psum(gram, "dom") / (ndom * node_dev)
    density = pl.pallas_call(
        density_kernel,
        name="density",
        out_shape=density_shape,
        in_specs=[vm] * 3,
        out_specs=vm,
        scratch_shapes=[pltpu.VMEM((orbs, 2 * orbs), F32), pltpu.VMEM((orbs, orbs), F32)],
        compiler_params=pltpu.CompilerParams(vmem_limit_bytes=VLIMIT),
    )(gram, quad, occ)
    return density.T


def solution(mesh):
    in_specs = (
        P("orb", "dom"),
        P(None, "dom"),
        P("dom"),
        P("dom"),
        P(None, "dom"),
        P("dom"),
        P(),
        P(),
        P("orb"),
        P(),
    )
    out_specs = P(None, "dom")
    return jax.shard_map(
        functools.partial(per_device, mesh.shape["dom"]),
        mesh=mesh,
        in_specs=in_specs,
        out_specs=out_specs,
        check_vma=False,
    )
```
